512 devices in a mesh: tok: 8 (over y), head: 8 (over z_lo, core), wid: 8 (over x, z_hi).
Axes of the slice: x: 4, y: 8, z: 8 (z_hi: 2, z_lo: 4; z = z_hi * 4 + z_lo), core: 2. Of those that a mesh axis runs over, the one named last changes fastest.
Arguments:
- inputs: bfloat16 [4096, 8192], P('tok', 'wid'), may hold values from -3 to 3
- q_grad: bfloat16 [4096, 8192], P(('tok', 'wid'), 'head'), may hold values from -0.59765625 to 0.59765625
- key_value_share_gradient: bfloat16 [4096, 2048], P(('tok', 'wid'), 'head'), may hold values from -0.59765625 to 0.59765625
- q_weight: bfloat16 [8192, 8192], P('wid', 'head'), may hold values from -0.59765625 to 0.59765625
- key_value_weight: bfloat16 [8192, 1024], P('wid', 'head'), may hold values from -0.59765625 to 0.59765625
Outputs:
- input_grad: bfloat16 [4096, 8192], P('tok', ('wid', 'head'))
- q_weight_grad: float32 [8192, 8192], P(('wid', 'tok'), 'head')
- kv_weight_grad: float32 [8192, 1024], P(('wid', 'tok'), 'head')
The draws below stay inside these ranges and needn't reach their ends.
All inputs are finite; a program needn't handle non-finite values.
Results may differ from the reference program's by a relative error of at most 0.017.
Values may be sent and summed in bfloat16 or wider, within the bound.
No kernel may reach another device: no remote copies, remote signals or barrier semaphores. Data moves between devices by JAX's collectives and lax.ppermute only.
A program may use at most 64 MiB of HBM per device.

```python
import jax
import jax.numpy as jnp
from jax import lax

MODEL_WIDTH = 8192
HEAD_SIZE = 128
QH_POS = 8
TOK_DEV = 512
HQ = 64
KEY_VALUE_HEADS = 4
TOTAL_TOKENS = 4096
N_TOK = 8
N_HEAD = 8


def strengthened(array, key, source, target, blocks, factor):
    def block_of(axis_at):
        return (jnp.arange(array.shape[axis_at]) // (array.shape[axis_at] // blocks)).reshape((-1,) + (1,) * (array.ndim - 1 - axis_at))

    one_side = jax.random.permutation(key, blocks)[block_of(target)]
    far = (block_of(target) + blocks // 2) % blocks
    return jnp.where((block_of(source) == one_side) | (block_of(source) == far), factor * array, array)


def shard_levels(own_key, extent, cuts, low, high):
    def one(dim, shards_of):
        steps = jax.random.uniform(jax.random.fold_in(jax.random.fold_in(own_key, 6), dim), (shards_of,), jnp.float32, low / len(cuts), high / len(cuts))
        return jnp.repeat(jnp.exp(steps), extent[dim] // shards_of).reshape((-1,) + (1,) * (len(extent) - dim - 1))

    loudness = one(*cuts[0])
    for cut in cuts[1:]:
        loudness = loudness * one(*cut)
    return loudness


def scatter_about(key, shape, deviation, reach, split=(), dtype=jnp.bfloat16):
    entries = jax.random.normal(key, shape, jnp.float32) * deviation
    if len(split) > 0:
        entries = shard_levels(key, shape, split, -0.22, 0.18) * entries
    return jnp.clip(entries, min=-reach, max=reach).astype(dtype)


def gaussian_with(stream_key, shape, deviation, most, cuts, heavy, held_as=jnp.bfloat16):
    values = deviation * jax.random.normal(stream_key, shape, jnp.float32)
    if cuts:
        values = values * shard_levels(stream_key, shape, cuts, -0.22, 0.18)
    return jnp.clip(strengthened(values, jax.random.fold_in(stream_key, 3), *heavy), -most, most).astype(held_as)


def setup_inputs(seed: int = 0) -> dict:
    key_of = jax.random.split(jax.random.key(seed), 6)
    return {
        "inputs": gaussian_with(key_of[0], (TOTAL_TOKENS, MODEL_WIDTH), 0.5, 3.0, ((0, 8), (1, 8)), (0, 1, 8, 2.0)),
        "q_grad": scatter_about(key_of[1], (TOTAL_TOKENS, HQ * HEAD_SIZE), 0.1, 0.59765625, ((0, 64), (1, 8))),
        "key_value_share_gradient": scatter_about(key_of[2], (TOTAL_TOKENS, KEY_VALUE_HEADS * 4 * HEAD_SIZE), 0.1, 0.59765625, ((0, 64), (1, 8))),
        "q_weight": scatter_about(key_of[3], (MODEL_WIDTH, HQ * HEAD_SIZE), 0.1, 0.59765625, ((0, 8), (1, 8))),
        "key_value_weight": scatter_about(key_of[4], (MODEL_WIDTH, KEY_VALUE_HEADS * 2 * HEAD_SIZE), 0.1, 0.59765625, ((0, 8), (1, 8))),
    }


def reference(inputs, q_grad, key_value_share_gradient, q_weight, key_value_weight):
    part_grads = key_value_share_gradient.astype(jnp.float32).reshape(TOTAL_TOKENS, N_HEAD // 2, 2, 2 * HEAD_SIZE)
    kv_full = (part_grads[:, :, 0] + part_grads[:, :, 1]).reshape(TOTAL_TOKENS, N_HEAD * HEAD_SIZE).astype(jnp.bfloat16)
    q_width = QH_POS * HEAD_SIZE

    def add_position(position, running):
        q_first = (position * q_width).astype(jnp.int32)
        kv_first = (position * HEAD_SIZE).astype(jnp.int32)
        grad_slice = lax.dynamic_slice_in_dim(q_grad, q_first, q_width, 1)
        weight_piece = lax.dynamic_slice_in_dim(q_weight, q_first, q_width, 1)
        kv_slice = lax.dynamic_slice_in_dim(kv_full, kv_first, HEAD_SIZE, 1)
        kv_weight_slice = lax.dynamic_slice_in_dim(key_value_weight, kv_first, HEAD_SIZE, 1)
        partial_term = jnp.dot(grad_slice, weight_piece.T, preferred_element_type=jnp.float32)
        partial_term = partial_term + jnp.dot(kv_slice, kv_weight_slice.T, preferred_element_type=jnp.float32)
        return running + lax.optimization_barrier(partial_term.astype(jnp.bfloat16)).astype(jnp.float32)

    input_sum = lax.fori_loop(0, N_HEAD, add_position, jnp.zeros((TOTAL_TOKENS, MODEL_WIDTH), jnp.float32))
    combined = jnp.concatenate([q_grad, kv_full], axis=1)

    def add_block(block_index, running):
        first_row = (block_index * TOK_DEV).astype(jnp.int32)
        token_rows = lax.dynamic_slice_in_dim(inputs, first_row, TOK_DEV, 0)
        grad_rows = lax.dynamic_slice_in_dim(combined, first_row, TOK_DEV, 0)
        partial_term = jnp.dot(token_rows.T, grad_rows, preferred_element_type=jnp.float32)
        return running + lax.optimization_barrier(partial_term.astype(jnp.bfloat16)).astype(jnp.float32)

    weight_sum = lax.fori_loop(0, N_TOK, add_block, jnp.zeros((MODEL_WIDTH, HQ * HEAD_SIZE + N_HEAD * HEAD_SIZE), jnp.float32))
    return input_sum.astype(jnp.bfloat16), weight_sum[:, :HQ * HEAD_SIZE], weight_sum[:, HQ * HEAD_SIZE:]
```

```python
import jax
import jax.numpy as jnp
from jax import lax
from jax.sharding import Mesh
from jax.sharding import PartitionSpec as P

SWAP = [(0, 1), (1, 0)]


def spread(rows):
    n = lax.axis_size("x")
    copies = jnp.broadcast_to(rows[None], (n, *rows.shape))
    return lax.all_to_all(copies, "x", 0, 0, tiled=True)


def contract_last(left, right):
    return lax.dot_general(
        left, right, (((1,), (1,)), ((), ())), preferred_element_type=jnp.float32
    )


def contract_first(left, right):
    return lax.dot_general(
        left, right, (((0,), (0,)), ((), ())), preferred_element_type=jnp.float32
    )


def local(inputs, q_grad, key_value_share_gradient, q_weight, key_value_weight):
    head_dim = key_value_weight.shape[1]
    q_columns = q_grad.shape[1]
    core = lax.axis_index("core")
    zhi = lax.axis_index("zhi")
    n_zlo = lax.axis_size("zlo")

    share = key_value_share_gradient
    outgoing = lax.dynamic_slice_in_dim(share, (1 - core) * head_dim, head_dim, 1)
    incoming = lax.ppermute(outgoing, "core", SWAP)
    own_part = lax.dynamic_slice_in_dim(share, core * head_dim, head_dim, 1)
    kv_rows = (own_part.astype(jnp.float32) + incoming.astype(jnp.float32)).astype(jnp.bfloat16)
    mine = jnp.concatenate([q_grad, kv_rows], axis=1)

    far = lax.ppermute(mine, "zhi", SWAP)
    near_all = spread(mine)
    far_all = spread(far)
    first = jnp.where(zhi == 0, near_all, far_all)
    second = jnp.where(zhi == 0, far_all, near_all)
    combined = jnp.stack([first, second], axis=1).reshape(-1, mine.shape[1])

    reduced = lax.psum_scatter(
        contract_first(inputs, combined).astype(jnp.bfloat16),
        "tok",
        scatter_dimension=0,
        tiled=True,
    ).astype(jnp.float32)

    weight = jnp.concatenate([q_weight, key_value_weight], axis=1)
    width = weight.shape[0] // (2 * n_zlo)
    weight = weight.reshape(n_zlo, 2, width, weight.shape[1])
    keep = lax.dynamic_index_in_dim(weight, core, 1, keepdims=False)
    give = lax.dynamic_index_in_dim(weight, 1 - core, 1, keepdims=False)

    def terms(part):
        return contract_last(combined, part.reshape(-1, part.shape[-1]))

    got = lax.ppermute(terms(give).astype(jnp.bfloat16), "core", SWAP)
    pair = (terms(keep) + got.astype(jnp.float32)).astype(jnp.bfloat16)
    pieces = jnp.swapaxes(pair.reshape(-1, n_zlo, width), 0, 1)
    pieces = lax.all_to_all(pieces, "zlo", 0, 0, tiled=True)
    input_grad = jnp.sum(pieces.astype(jnp.float32), axis=0).astype(jnp.bfloat16)
    return (input_grad, reduced[:, :q_columns], reduced[:, q_columns:])


def solution(mesh):
    fine = Mesh(
        mesh.devices.reshape(8, 4, 2, 4, 2), ("tok", "zlo", "core", "x", "zhi")
    )
    tok, head, wid = "tok", ("zlo", "core"), ("x", "zhi")
    return jax.shard_map(
        local,
        mesh=fine,
        in_specs=(
            P(tok, wid),
            P((tok, *wid), head),
            P((tok, *wid), head),
            P(wid, head),
            P(wid, head),
        ),
        out_specs=(P(tok, (*wid, *head)), P((*wid, tok), head), P((*wid, tok), head)),
        check_vma=False,
    )
```

```python
import jax
import jax.numpy as jnp
from jax import lax
from jax.sharding import Mesh
from jax.sharding import PartitionSpec as P

SWAP = [(0, 1), (1, 0)]
WID = ("x", "zhi")
TOK = ("th", "tl")
HEAD = ("zlo", "core")
CHUNKS = (384, 384, 384)


def neighbour(at):
    y, core = divmod(at, 2)
    other = y ^ 1 if core == 0 else (y + (1 if y % 2 else -1)) % 8
    return other * 2 + core


NEIGHBOUR = [(i, neighbour(i)) for i in range(16)]


def spread(rows):
    n = lax.axis_size(WID)
    copies = jnp.broadcast_to(rows[None], (n, *rows.shape))
    return lax.all_to_all(copies, WID, 0, 0, tiled=True).reshape(-1, rows.shape[1])


def contract_last(left, right):
    return lax.dot_general(
        left, right, (((1,), (1,)), ((), ())), preferred_element_type=jnp.float32
    )


def matmul(left, right):
    return jnp.dot(left, right, preferred_element_type=jnp.float32)


def local(inputs, q_grad, key_value_share_gradient, q_weight, key_value_weight):
    head_dim = key_value_weight.shape[1]
    q_columns = q_grad.shape[1]
    core = lax.axis_index("core")
    tl = lax.axis_index("tl")
    n_zlo, n_th = lax.axis_size("zlo"), lax.axis_size("th")

    share = key_value_share_gradient
    outgoing = lax.dynamic_slice_in_dim(share, (1 - core) * head_dim, head_dim, 1)
    incoming = lax.ppermute(outgoing, "core", SWAP)
    own_part = lax.dynamic_slice_in_dim(share, core * head_dim, head_dim, 1)
    kv_rows = (own_part.astype(jnp.float32) + incoming.astype(jnp.float32)).astype(jnp.bfloat16)

    chunks = []
    at = 0
    for size in CHUNKS[:-1]:
        chunks.append(spread(q_grad[:, at : at + size]))
        at += size
    chunks.append(spread(jnp.concatenate([q_grad[:, at:], kv_rows], axis=1)))

    flipped = inputs.T
    tall = flipped.shape[0] // (2 * n_th)
    flipped = flipped.reshape(n_th, 2, tall, -1)
    keep_in = lax.dynamic_index_in_dim(flipped, tl, 1, keepdims=False).reshape(n_th * tall, -1)
    give_in = lax.dynamic_index_in_dim(flipped, 1 - tl, 1, keepdims=False).reshape(n_th * tall, -1)

    sums = []
    for chunk in chunks:
        give = matmul(give_in, chunk).astype(jnp.bfloat16)
        got = lax.ppermute(give, (*TOK, "core"), NEIGHBOUR)
        pair = (matmul(keep_in, chunk) + got.astype(jnp.float32)).astype(jnp.bfloat16)
        pieces = lax.all_to_all(pair.reshape(n_th, tall, -1), "th", 0, 0, tiled=True)
        sums.append(jnp.sum(pieces.astype(jnp.float32), axis=0))

    combined = jnp.concatenate(chunks, axis=1)
    weight = jnp.concatenate([q_weight, key_value_weight], axis=1)
    width = weight.shape[0] // (2 * n_zlo)
    weight = weight.reshape(n_zlo, 2, width, weight.shape[1])
    keep_w = lax.dynamic_index_in_dim(weight, core, 1, keepdims=False)
    give_w = lax.dynamic_index_in_dim(weight, 1 - core, 1, keepdims=False)

    def terms(part):
        return contract_last(combined, part.reshape(-1, part.shape[-1]))

    got = lax.ppermute(terms(give_w).astype(jnp.bfloat16), "core", SWAP)
    pair = (terms(keep_w) + got.astype(jnp.float32)).astype(jnp.bfloat16)
    pieces = jnp.swapaxes(pair.reshape(-1, n_zlo, width), 0, 1)
    pieces = lax.all_to_all(pieces, "zlo", 0, 0, tiled=True)
    input_grad = jnp.sum(pieces.astype(jnp.float32), axis=0).astype(jnp.bfloat16)

    last = q_columns - sum(CHUNKS[:-1])
    q_out = jnp.concatenate([*sums[:-1], sums[-1][:, :last]], axis=1)
    return (input_grad, q_out, sums[-1][:, last:])


def solution(mesh):
    fine = Mesh(
        mesh.devices.reshape(4, 2, 4, 2, 4, 2), ("th", "tl", "zlo", "core", "x", "zhi")
    )
    return jax.shard_map(
        local,
        mesh=fine,
        in_specs=(
            P(TOK, WID),
            P((*TOK, *WID), HEAD),
            P((*TOK, *WID), HEAD),
            P(WID, HEAD),
            P(WID, HEAD),
        ),
        out_specs=(P(TOK, (*WID, *HEAD)), P((*WID, *TOK), HEAD), P((*WID, *TOK), HEAD)),
        check_vma=False,
    )
```

```python
import jax
import jax.numpy as jnp
from jax import lax
from jax.sharding import Mesh
from jax.sharding import PartitionSpec as P

SWAP = [(0, 1), (1, 0)]
WID = ("x", "zhi")
TOK = ("th", "tl")
HEAD = ("zlo", "core")


def neighbour(at):
    y, core = divmod(at, 2)
    other = y ^ 1 if core == 0 else (y + (1 if y % 2 else -1)) % 8
    return other * 2 + core


NEIGHBOUR = [(i, neighbour(i)) for i in range(16)]


def spread(rows):
    n = lax.axis_size("x")
    copies = jnp.broadcast_to(rows[None], (n, *rows.shape))
    return lax.all_to_all(copies, "x", 0, 0, tiled=True)


def contract_last(left, right):
    return lax.dot_general(
        left, right, (((1,), (1,)), ((), ())), preferred_element_type=jnp.float32
    )


def matmul(left, right):
    return jnp.dot(left, right, preferred_element_type=jnp.float32)


def halves(rows, which, n):
    pairs = rows.reshape(n, 2, rows.shape[0] // (2 * n), rows.shape[1])
    keep = lax.dynamic_index_in_dim(pairs, which, 1, keepdims=False)
    give = lax.dynamic_index_in_dim(pairs, 1 - which, 1, keepdims=False)
    return keep.reshape(-1, rows.shape[1]), give.reshape(-1, rows.shape[1])


def local(inputs, q_grad, key_value_share_gradient, q_weight, key_value_weight):
    head_dim = key_value_weight.shape[1]
    q_columns = q_grad.shape[1]
    core = lax.axis_index("core")
    tl = lax.axis_index("tl")
    zhi = lax.axis_index("zhi")
    n_zlo, n_th = lax.axis_size("zlo"), lax.axis_size("th")

    share = key_value_share_gradient
    outgoing = lax.dynamic_slice_in_dim(share, (1 - core) * head_dim, head_dim, 1)
    incoming = lax.ppermute(outgoing, "core", SWAP)
    own_part = lax.dynamic_slice_in_dim(share, core * head_dim, head_dim, 1)
    kv_rows = (own_part.astype(jnp.float32) + incoming.astype(jnp.float32)).astype(jnp.bfloat16)
    mine = jnp.concatenate([q_grad, kv_rows], axis=1)

    far = lax.ppermute(mine, "zhi", SWAP)
    near_all = spread(mine)
    far_all = spread(far)
    first = jnp.where(zhi == 0, near_all, far_all)
    second = jnp.where(zhi == 0, far_all, near_all)
    combined = jnp.stack([first, second], axis=1).reshape(-1, mine.shape[1])

    keep_in, give_in = halves(inputs.T, tl, n_th)
    given = matmul(give_in, combined).astype(jnp.bfloat16)
    got = lax.ppermute(given, (*TOK, "core"), NEIGHBOUR)

    keep_q, give_q = halves(q_weight, core, n_zlo)
    keep_kv, give_kv = halves(key_value_weight, core, n_zlo)
    q_rows, kv_rows = combined[:, :q_columns], combined[:, q_columns:]

    def terms(q_part, kv_part):
        return contract_last(q_part, q_rows) + contract_last(kv_part, kv_rows)

    core_got = lax.ppermute(terms(give_q, give_kv).astype(jnp.bfloat16), "core", SWAP)
    pair = (terms(keep_q, keep_kv) + core_got.astype(jnp.float32)).astype(jnp.bfloat16)
    pieces = lax.all_to_all(pair.reshape(n_zlo, -1, pair.shape[1]), "zlo", 0, 0, tiled=True)
    input_grad = jnp.sum(pieces.astype(jnp.float32), axis=0).T.astype(jnp.bfloat16)

    pair = (matmul(keep_in, combined) + got.astype(jnp.float32)).astype(jnp.bfloat16)
    pieces = lax.all_to_all(pair.reshape(n_th, -1, pair.shape[1]), "th", 0, 0, tiled=True)
    total = jnp.sum(pieces.astype(jnp.float32), axis=0)
    return (input_grad, total[:, :q_columns], total[:, q_columns:])


def solution(mesh):
    fine = Mesh(
        mesh.devices.reshape(4, 2, 4, 2, 4, 2), ("th", "tl", "zlo", "core", "x", "zhi")
    )
    return jax.shard_map(
        local,
        mesh=fine,
        in_specs=(
            P(TOK, WID),
            P((*TOK, *WID), HEAD),
            P((*TOK, *WID), HEAD),
            P(WID, HEAD),
            P(WID, HEAD),
        ),
        out_specs=(P(TOK, (*WID, *HEAD)), P((*WID, *TOK), HEAD), P((*WID, *TOK), HEAD)),
        check_vma=False,
    )
```

```python
import functools

import jax
import jax.numpy as jnp
from jax import lax
from jax.experimental import pallas as pl
from jax.experimental.pallas import tpu as pltpu
from jax.sharding import Mesh
from jax.sharding import PartitionSpec as P

SWAP = [(0, 1), (1, 0)]
WID = ("x", "zhi")
TOK = ("th", "tl")
HEAD = ("zlo", "core")
N_Y = 8
N_PAIRS = 4
VMEM_LIMIT = 48 * 2**20


def side(y, core):
    return 2 * ((y + core) % 2) - 1


def moved(step):
    return [
        (y * 2 + core, (y + step(y, core)) % N_Y * 2 + core)
        for y in range(N_Y)
        for core in range(2)
    ]


def spread(rows):
    n = lax.axis_size("x")
    copies = jnp.broadcast_to(rows[None], (n, *rows.shape))
    return lax.all_to_all(copies, "x", 0, 0, tiled=True)


def dot(left, right, dims):
    return lax.dot_general(left, right, ((dims[:1], dims[1:]), ((), ())), preferred_element_type=jnp.float32)


def weight_body(blocks, x_ref, g_ref, *refs):
    for r in range(N_PAIRS):
        columns = x_ref[:, pl.ds(pl.multiple_of(blocks[r] * 128, 128), 128)]
        term = dot(columns, g_ref[...], (0, 0))
        if len(refs) == 1:
            refs[0][r] = term.astype(jnp.bfloat16)
        else:
            refs[1 + r][...] = (term + refs[0][r].astype(jnp.float32)).astype(jnp.bfloat16)


def weight_terms(blocks, x, g, got=None):
    extra = () if got is None else (got,)
    vmem = pl.BlockSpec(memory_space=pltpu.VMEM)
    if got is None:
        shapes = [jax.ShapeDtypeStruct((N_PAIRS, 128, g.shape[1]), jnp.bfloat16)]
    else:
        shapes = [jax.ShapeDtypeStruct((128, g.shape[1]), jnp.bfloat16)] * N_PAIRS
    return pl.pallas_call(
        weight_body,
        out_shape=shapes,
        in_specs=[pl.BlockSpec(memory_space=pltpu.SMEM)] + [vmem] * (2 + len(extra)),
        out_specs=[vmem] * len(shapes),
        compiler_params=pltpu.CompilerParams(vmem_limit_bytes=VMEM_LIMIT),
        cost_estimate=pl.CostEstimate(
            flops=2 * 512 * 512 * g.shape[1], bytes_accessed=4 * 2**20, transcendentals=0
        ),
    )(blocks, x, g, *extra)


def input_body(which, g_ref, wq_ref, wkv_ref, *refs):
    out = refs[-1]
    n_q = wq_ref.shape[-1]
    term = dot(g_ref[:, :n_q], wq_ref[0], (1, 1))
    term = term + dot(g_ref[:, n_q:], wkv_ref[0], (1, 1))
    if len(refs) > 1:
        term = term + refs[0][0].astype(jnp.float32)
    out[0] = term.astype(out.dtype)


def input_terms(which, g, wq, wkv, got=None):
    n_q, n_kv = wq.shape[1], wkv.shape[1]
    n = wq.shape[0] // 256
    rows = g.shape[0]
    whole = lambda r, which: (0, 0)
    pick = lambda r, which: (2 * r + which[0], 0, 0)
    mine = lambda r, which: (r, 0, 0)
    extra = () if got is None else (got,)
    return pl.pallas_call(
        input_body,
        grid_spec=pltpu.PrefetchScalarGridSpec(
            num_scalar_prefetch=1,
            grid=(n,),
            in_specs=[
                pl.BlockSpec(g.shape, whole),
                pl.BlockSpec((1, 128, n_q), pick),
                pl.BlockSpec((1, 128, n_kv), pick),
            ]
            + [pl.BlockSpec((1, rows, 128), mine)] * len(extra),
            out_specs=pl.BlockSpec((1, rows, 128), mine),
        ),
        out_shape=jax.ShapeDtypeStruct((n, rows, 128), jnp.bfloat16),
        compiler_params=pltpu.CompilerParams(vmem_limit_bytes=VMEM_LIMIT),
        cost_estimate=pl.CostEstimate(
            flops=2 * 512 * 512 * 1152, bytes_accessed=4 * 2**20, transcendentals=0
        ),
    )(which, g, wq.reshape(-1, 128, n_q), wkv.reshape(-1, 128, n_kv), *extra)


def local(inputs, q_grad, key_value_share_gradient, q_weight, key_value_weight):
    head_dim = key_value_weight.shape[1]
    q_columns = q_grad.shape[1]
    core = lax.axis_index("core")
    zhi = lax.axis_index("zhi")
    y = lax.axis_index(TOK)

    share = key_value_share_gradient
    outgoing = lax.dynamic_slice_in_dim(share, (1 - core) * head_dim, head_dim, 1)
    incoming = lax.ppermute(outgoing, "core", SWAP)
    own_part = lax.dynamic_slice_in_dim(share, core * head_dim, head_dim, 1)
    kv_rows = (own_part.astype(jnp.float32) + incoming.astype(jnp.float32)).astype(jnp.bfloat16)
    mine = jnp.concatenate([q_grad, kv_rows], axis=1)

    sigma = side(y, core)
    steps = jnp.arange(N_PAIRS, dtype=jnp.int32)
    keep_blocks = (y + sigma * steps) % N_Y
    give_blocks = (y - sigma * (1 + steps)) % N_Y
    give_which = (1 - core).reshape(1)
    keep_which = core.reshape(1)

    far = lax.ppermute(mine, "zhi", SWAP)
    near_all = spread(mine)
    far, near_all, near_first, keep_blocks, give_blocks, keep_which, give_which = (
        lax.optimization_barrier(
            (far, near_all, zhi == 0, keep_blocks, give_blocks, keep_which, give_which)
        )
    )
    far_all = spread(far)
    first = jnp.where(near_first, near_all, far_all)
    second = jnp.where(near_first, far_all, near_all)
    combined = jnp.stack([first, second], axis=1).reshape(-1, mine.shape[1])

    (given,) = weight_terms(give_blocks, inputs, combined)
    got = lax.ppermute(given, (*TOK, "core"), moved(lambda y, core: -side(y, core)))

    core_got = lax.ppermute(input_terms(give_which, combined, q_weight, key_value_weight), "core", SWAP)
    pieces = input_terms(keep_which, combined, q_weight, key_value_weight, core_got)
    pieces = lax.all_to_all(pieces, "zlo", 0, 0, tiled=True)
    input_grad = jnp.sum(pieces.astype(jnp.float32), axis=0).astype(jnp.bfloat16)

    kept = weight_terms(keep_blocks, inputs, combined, got)
    pieces = [
        lax.ppermute(kept[r], (*TOK, "core"), moved(lambda y, core: r * side(y, core)))
        for r in range(N_PAIRS - 1, 0, -1)
    ]

    def total(columns):
        return sum(piece[:, columns].astype(jnp.float32) for piece in [kept[0], *pieces])

    return (input_grad, total(slice(0, q_columns)), total(slice(q_columns, None)))


def solution(mesh):
    fine = Mesh(
        mesh.devices.reshape(4, 2, 4, 2, 4, 2), ("th", "tl", "zlo", "core", "x", "zhi")
    )
    return jax.shard_map(
        local,
        mesh=fine,
        in_specs=(
            P(TOK, WID),
            P((*TOK, *WID), HEAD),
            P((*TOK, *WID), HEAD),
            P(WID, HEAD),
            P(WID, HEAD),
        ),
        out_specs=(P(TOK, (*WID, *HEAD)), P((*WID, *TOK), HEAD), P((*WID, *TOK), HEAD)),
        check_vma=False,
    )
```

```python
import functools

import jax
import jax.numpy as jnp
from jax import lax
from jax.experimental import pallas as pl
from jax.experimental.pallas import tpu as pltpu
from jax.sharding import Mesh
from jax.sharding import PartitionSpec as P

SWAP = [(0, 1), (1, 0)]
CROSS = [(0, 3), (1, 2), (2, 1), (3, 0)]
WID = ("x", "zhi")
TOK = ("th", "tl")
HEAD = ("zlo", "core")
N_Y = 8
N_PAIRS = 4
VMEM_LIMIT = 48 * 2**20


def side(y, core):
    return 2 * ((y + core) % 2) - 1


def moved(step):
    return [
        (y * 2 + core, (y + step(y, core)) % N_Y * 2 + core)
        for y in range(N_Y)
        for core in range(2)
    ]


def spread(rows):
    n = lax.axis_size("x")
    copies = jnp.broadcast_to(rows[None], (n, *rows.shape))
    return lax.all_to_all(copies, "x", 0, 0, tiled=True)


def dot(left, right, dims):
    return lax.dot_general(left, right, ((dims[:1], dims[1:]), ((), ())), preferred_element_type=jnp.float32)


def weight_body(blocks, x_ref, g_ref, *refs):
    for r in range(N_PAIRS):
        columns = x_ref[:, pl.ds(pl.multiple_of(blocks[r] * 128, 128), 128)]
        term = dot(columns, g_ref[...], (0, 0))
        if len(refs) == 1:
            refs[0][r] = term.astype(jnp.bfloat16)
        else:
            refs[1 + r][...] = (term + refs[0][r].astype(jnp.float32)).astype(jnp.bfloat16)


def weight_terms(blocks, x, g, got=None):
    extra = () if got is None else (got,)
    vmem = pl.BlockSpec(memory_space=pltpu.VMEM)
    if got is None:
        shapes = [jax.ShapeDtypeStruct((N_PAIRS, 128, g.shape[1]), jnp.bfloat16)]
    else:
        shapes = [jax.ShapeDtypeStruct((128, g.shape[1]), jnp.bfloat16)] * N_PAIRS
    return pl.pallas_call(
        weight_body,
        out_shape=shapes,
        in_specs=[pl.BlockSpec(memory_space=pltpu.SMEM)] + [vmem] * (2 + len(extra)),
        out_specs=[vmem] * len(shapes),
        compiler_params=pltpu.CompilerParams(vmem_limit_bytes=VMEM_LIMIT),
        cost_estimate=pl.CostEstimate(
            flops=2 * 512 * 512 * g.shape[1], bytes_accessed=4 * 2**20, transcendentals=0
        ),
    )(blocks, x, g, *extra)


def sum_body(*refs):
    *pieces, q_ref, kv_ref = refs
    n_q = q_ref.shape[1]
    q_ref[...] = sum(piece[:, :n_q].astype(jnp.float32) for piece in pieces)
    kv_ref[...] = sum(piece[:, n_q:].astype(jnp.float32) for piece in pieces)


def last_sum(pieces, n_q):
    rows, columns = pieces[0].shape
    step = rows // 2
    block = lambda width: pl.BlockSpec((step, width), lambda i: (i, 0))
    return pl.pallas_call(
        sum_body,
        grid=(2,),
        out_shape=[
            jax.ShapeDtypeStruct((rows, n_q), jnp.float32),
            jax.ShapeDtypeStruct((rows, columns - n_q), jnp.float32),
        ],
        in_specs=[block(columns)] * len(pieces),
        out_specs=[block(n_q), block(columns - n_q)],
        compiler_params=pltpu.CompilerParams(vmem_limit_bytes=VMEM_LIMIT),
        cost_estimate=pl.CostEstimate(
            flops=4 * rows * columns, bytes_accessed=12 * rows * columns, transcendentals=0
        ),
    )(*pieces)


def input_body(which, g_ref, wq_ref, wkv_ref, *refs):
    out = refs[-1]
    n_q = wq_ref.shape[-1]
    term = dot(g_ref[:, :n_q], wq_ref[0], (1, 1))
    term = term + dot(g_ref[:, n_q:], wkv_ref[0], (1, 1))
    if len(refs) > 1:
        term = term + refs[0][0].astype(jnp.float32)
    out[0] = term.astype(out.dtype)


def input_terms(which, g, wq, wkv, got=None):
    n_q, n_kv = wq.shape[1], wkv.shape[1]
    n = wq.shape[0] // 256
    rows = g.shape[0]
    whole = lambda r, which: (0, 0)
    pick = lambda r, which: (2 * r + which[0], 0, 0)
    mine = lambda r, which: (r, 0, 0)
    extra = () if got is None else (got,)
    return pl.pallas_call(
        input_body,
        grid_spec=pltpu.PrefetchScalarGridSpec(
            num_scalar_prefetch=1,
            grid=(n,),
            in_specs=[
                pl.BlockSpec(g.shape, whole),
                pl.BlockSpec((1, 128, n_q), pick),
                pl.BlockSpec((1, 128, n_kv), pick),
            ]
            + [pl.BlockSpec((1, rows, 128), mine)] * len(extra),
            out_specs=pl.BlockSpec((1, rows, 128), mine),
        ),
        out_shape=jax.ShapeDtypeStruct((n, rows, 128), jnp.bfloat16),
        compiler_params=pltpu.CompilerParams(vmem_limit_bytes=VMEM_LIMIT),
        cost_estimate=pl.CostEstimate(
            flops=2 * 512 * 512 * 1152, bytes_accessed=4 * 2**20, transcendentals=0
        ),
    )(which, g, wq.reshape(-1, 128, n_q), wkv.reshape(-1, 128, n_kv), *extra)


def local(inputs, q_grad, key_value_share_gradient, q_weight, key_value_weight):
    head_dim = key_value_weight.shape[1]
    q_columns = q_grad.shape[1]
    core = lax.axis_index("core")
    zhi = lax.axis_index("zhi")
    y = lax.axis_index(TOK)

    share = key_value_share_gradient
    outgoing = lax.dynamic_slice_in_dim(share, (1 - core) * head_dim, head_dim, 1)
    own_part = lax.dynamic_slice_in_dim(share, core * head_dim, head_dim, 1)
    mine = jnp.concatenate([q_grad, own_part], axis=1)
    mine, outgoing = lax.optimization_barrier((mine, outgoing))
    part = lax.ppermute(outgoing, "core", SWAP)
    far_part = lax.ppermute(outgoing, ("core", "zhi"), CROSS)
    far = lax.ppermute(mine, "zhi", SWAP)

    sigma = side(y, core)
    steps = jnp.arange(N_PAIRS, dtype=jnp.int32)
    keep_blocks = (y + sigma * steps) % N_Y
    give_blocks = (y - sigma * (1 + steps)) % N_Y
    give_which = (1 - core).reshape(1)
    keep_which = core.reshape(1)
    near_first = zhi == 0
    orders = (near_first, keep_blocks, give_blocks, keep_which, give_which)
    far, far_part, part, mine, orders = lax.optimization_barrier((far, far_part, part, mine, orders))
    near_first, keep_blocks, give_blocks, keep_which, give_which = orders

    def with_sum(rows, more):
        kv_rows = rows[:, q_columns:].astype(jnp.float32) + more.astype(jnp.float32)
        return rows[:, :q_columns], kv_rows.astype(jnp.bfloat16)

    def in_order(one, other):
        return jnp.concatenate(
            [jnp.where(near_first, one, other), jnp.where(near_first, other, one)]
        )

    both = [in_order(one, other) for one, other in zip(with_sum(mine, part), with_sum(far, far_part))]
    combined = spread(jnp.concatenate(both, axis=1))
    combined = combined.reshape(-1, mine.shape[1])

    (given,) = weight_terms(give_blocks, inputs, combined)
    got = lax.ppermute(given, (*TOK, "core"), moved(lambda y, core: -side(y, core)))
    kept = weight_terms(keep_blocks, inputs, combined, got)

    core_got = lax.ppermute(input_terms(give_which, combined, q_weight, key_value_weight), "core", SWAP)
    terms = input_terms(keep_which, combined, q_weight, key_value_weight, core_got)

    pieces = [kept[0]]
    for r in range(N_PAIRS - 1, 0, -1):
        piece = lax.ppermute(kept[r], (*TOK, "core"), moved(lambda y, core: r * side(y, core)))
        pieces.append(piece)
    terms = lax.all_to_all(terms, "zlo", 0, 0, tiled=True)
    input_grad = jnp.sum(terms.astype(jnp.float32), axis=0).astype(jnp.bfloat16)
    return (input_grad, *last_sum(pieces, q_columns))


def solution(mesh):
    fine = Mesh(
        mesh.devices.reshape(4, 2, 4, 2, 4, 2), ("th", "tl", "zlo", "core", "x", "zhi")
    )
    return jax.shard_map(
        local,
        mesh=fine,
        in_specs=(
            P(TOK, WID),
            P((*TOK, *WID), HEAD),
            P((*TOK, *WID), HEAD),
            P(WID, HEAD),
            P(WID, HEAD),
        ),
        out_specs=(P(TOK, (*WID, *HEAD)), P((*WID, *TOK), HEAD), P((*WID, *TOK), HEAD)),
        check_vma=False,
    )
```

```python
import functools

import jax
import jax.numpy as jnp
from jax import lax
from jax.experimental import pallas as pl
from jax.experimental.pallas import tpu as pltpu
from jax.sharding import Mesh
from jax.sharding import PartitionSpec as P

SWAP = [(0, 1), (1, 0)]
WID = ("x", "zhi")
TOK = ("th", "tl")
HEAD = ("zlo", "core")
N_Y = 8
N_PAIRS = 4
VMEM_LIMIT = 32 * 2**20
COST = pl.CostEstimate(flops=1, bytes_accessed=1, transcendentals=0)
LONG = pl.CostEstimate(flops=5 * 10**10, bytes_accessed=1, transcendentals=0)


def inner(v, where):
    return where((v % 4 == 1) | (v % 4 == 2), True, False)


def second(v, where):
    return where(inner(v, where), (3 - v) % N_Y, (7 - v) % N_Y)


def third(v, where):
    return where(inner(v, where), (7 - v) % N_Y, (3 - v) % N_Y)


def select(condition, one, other):
    return one if condition else other


def swapped(partner):
    return [
        ((v + core) % N_Y * 2 + core, (partner(v) + core) % N_Y * 2 + core)
        for v in range(N_Y)
        for core in range(2)
    ]


FIRST = swapped(lambda v: v ^ 1)
SECOND = swapped(lambda v: second(v, select))
THIRD = swapped(lambda v: third(v, select))
PARTS = (640, 512)


VMEM = pl.BlockSpec(memory_space=pltpu.VMEM)
SMEM = pl.BlockSpec(memory_space=pltpu.SMEM)
PARAMS = pltpu.CompilerParams(vmem_limit_bytes=VMEM_LIMIT)


def own_body(core, q_hbm, share_hbm, more_ref, out_ref, share_ref, sems):
    n_q = q_hbm.shape[1]
    q_copy = pltpu.make_async_copy(q_hbm, out_ref.at[:, pl.ds(0, n_q)], sems.at[0])
    share_copy = pltpu.make_async_copy(share_hbm, share_ref, sems.at[1])
    q_copy.start()
    share_copy.start()
    share_copy.wait()
    columns = pl.ds(pl.multiple_of(core[0] * 128, 128), 128)
    kv = share_ref[:, columns].astype(jnp.float32) + more_ref[:, columns].astype(jnp.float32)
    out_ref[:, n_q:] = kv.astype(out_ref.dtype)
    q_copy.wait()


def own_rows(core, q, share, more):
    hbm = pl.BlockSpec(memory_space=pltpu.HBM)
    return pl.pallas_call(
        own_body,
        out_shape=jax.ShapeDtypeStruct((q.shape[0], q.shape[1] + 128), q.dtype),
        in_specs=[SMEM, hbm, hbm, VMEM],
        out_specs=VMEM,
        scratch_shapes=[pltpu.VMEM(share.shape, share.dtype), pltpu.SemaphoreType.DMA((2,))],
        compiler_params=PARAMS,
        cost_estimate=COST,
    )(core, q, share, more)


def again_body(rows_ref, out_ref):
    out_ref[...] = rows_ref[...]


def again(rows):
    return pl.pallas_call(
        again_body,
        out_shape=jax.ShapeDtypeStruct(rows.shape, rows.dtype),
        in_specs=[VMEM],
        out_specs=VMEM,
        compiler_params=PARAMS,
        cost_estimate=LONG,
    )(rows)


def shifted(rows, by):
    n = lax.axis_size("x")
    return lax.ppermute(rows, "x", [(i, (i + by) % n) for i in range(n)])


def all_along_x(rows):
    moved_rows = {by: shifted(rows, by) for by in (1, 3, 2)}
    return [rows] + [moved_rows[by] for by in (1, 2, 3)]


def order_body(place, *refs):
    *parts, out_ref = refs
    n = len(parts) // 2
    x, zhi = place[0], place[1]
    for by in range(n):
        at = 2 * ((x + n - by) % n)
        out_ref[at + zhi] = parts[by][...]
        out_ref[at + 1 - zhi] = parts[n + by][...]


def in_order(place, near, far):
    rows, columns = near[0].shape
    parts = [*near, *far]
    return pl.pallas_call(
        order_body,
        out_shape=jax.ShapeDtypeStruct((len(parts), rows, columns), near[0].dtype),
        in_specs=[SMEM] + [VMEM] * len(parts),
        out_specs=VMEM,
        compiler_params=PARAMS,
        cost_estimate=COST,
    )(place, *parts).reshape(-1, columns)


def dot(left, right, dims):
    return lax.dot_general(left, right, ((dims[:1], dims[1:]), ((), ())), preferred_element_type=jnp.float32)


def give_body(blocks, x_ref, g_ref, *outs):
    for r in range(N_PAIRS):
        columns = x_ref[:, pl.ds(pl.multiple_of(blocks[r] * 128, 128), 128)]
        at = 0
        for out in outs:
            width = out.shape[-1]
            out[r] = dot(columns, g_ref[:, at : at + width], (0, 0)).astype(out.dtype)
            at += width


def give_terms(blocks, x, g):
    return pl.pallas_call(
        give_body,
        out_shape=[jax.ShapeDtypeStruct((N_PAIRS, 128, width), jnp.bfloat16) for width in PARTS],
        in_specs=[SMEM] + [VMEM] * 2,
        out_specs=[VMEM] * len(PARTS),
        compiler_params=PARAMS,
        cost_estimate=COST,
    )(blocks, x, g)


def keep_body(at, blocks, x_ref, g_ref, got_ref, give_ref, keep_ref):
    width = got_ref.shape[-1]
    for r in range(N_PAIRS):
        columns = x_ref[:, pl.ds(pl.multiple_of(blocks[r] * 128, 128), 128)]
        term = dot(columns, g_ref[:, at : at + width], (0, 0)) + got_ref[r].astype(jnp.float32)
        out = give_ref if r < 2 else keep_ref
        out[r % 2] = term.astype(out.dtype)


def keep_terms(blocks, x, g, got, at):
    return pl.pallas_call(
        functools.partial(keep_body, at),
        out_shape=[jax.ShapeDtypeStruct((2, *got.shape[1:]), jnp.bfloat16)] * 2,
        in_specs=[SMEM] + [VMEM] * 3,
        out_specs=[VMEM] * 2,
        compiler_params=PARAMS,
        cost_estimate=COST,
    )(blocks, x, g, got)


def add_body(*refs):
    *parts, keep_ref, give_ref = refs
    at = 0
    for kept, got in zip(parts[::2], parts[1::2]):
        width = kept.shape[-1]
        for r, out in enumerate((keep_ref, give_ref)):
            total = kept[r].astype(jnp.float32) + got[r].astype(jnp.float32)
            out[:, at : at + width] = total.astype(out.dtype)
        at += width


def add_terms(*parts):
    columns = sum(part.shape[-1] for part in parts[::2])
    return pl.pallas_call(
        add_body,
        out_shape=[jax.ShapeDtypeStruct((parts[0].shape[1], columns), jnp.bfloat16)] * 2,
        in_specs=[VMEM] * len(parts),
        out_specs=[VMEM] * 2,
        compiler_params=PARAMS,
        cost_estimate=COST,
    )(*parts)


def sum_body(input_kept, input_got, kept, got, input_out, q_ref, kv_ref):
    n_q = q_ref.shape[1]
    total = input_kept[...].astype(jnp.float32) + input_got[...].astype(jnp.float32)
    input_out[...] = total.astype(input_out.dtype)
    q_ref[...] = kept[:, :n_q].astype(jnp.float32) + got[:, :n_q].astype(jnp.float32)
    kv_ref[...] = kept[:, n_q:].astype(jnp.float32) + got[:, n_q:].astype(jnp.float32)


def last_sums(input_kept, input_got, kept, got, n_q):
    rows, columns = kept.shape
    outs = [
        jax.ShapeDtypeStruct(input_kept.shape, jnp.bfloat16),
        jax.ShapeDtypeStruct((rows, n_q), jnp.float32),
        jax.ShapeDtypeStruct((rows, columns - n_q), jnp.float32),
    ]
    block = lambda array: pl.BlockSpec(array.shape, lambda i: (0, 0))
    arrays = [input_kept, input_got, kept, got]
    return pl.pallas_call(
        sum_body,
        grid=(1,),
        out_shape=outs,
        in_specs=[block(array) for array in arrays],
        out_specs=[block(out) for out in outs],
        compiler_params=PARAMS,
        cost_estimate=COST,
    )(*arrays)


def input_body(blocks, g_ref, wq_ref, wkv_ref, *refs):
    n_q = wq_ref.shape[-1]
    term = dot(g_ref[:, :n_q], wq_ref[0], (1, 1))
    term = term + dot(g_ref[:, n_q:], wkv_ref[0], (1, 1))
    if len(refs) == 1:
        refs[0][0] = term.astype(jnp.bfloat16)
        return
    got_ref, *outs = refs
    term = (term + got_ref[0].astype(jnp.float32)).astype(jnp.bfloat16)
    for half, out in enumerate(outs):

        @pl.when(pl.program_id(0) // 2 == half)
        def _():
            out[0] = term


def input_terms(blocks, g, wq, wkv, *got):
    n_q, n_kv = wq.shape[1], wkv.shape[1]
    rows = g.shape[0]
    n = blocks.shape[0]
    pick = lambda r, blocks: (blocks[r], 0, 0)
    mine = lambda r, blocks: (r, 0, 0)
    block = (1, rows, 128)
    if got:
        places = [
            lambda r, blocks: (jnp.minimum(r, 1), 0, 0),
            lambda r, blocks: (jnp.maximum(r - 2, 0), 0, 0),
        ]
    else:
        places = [mine]
    return pl.pallas_call(
        input_body,
        grid_spec=pltpu.PrefetchScalarGridSpec(
            num_scalar_prefetch=1,
            grid=(n,),
            in_specs=[
                pl.BlockSpec(g.shape, lambda r, blocks: (0, 0)),
                pl.BlockSpec((1, 128, n_q), pick),
                pl.BlockSpec((1, 128, n_kv), pick),
            ]
            + [pl.BlockSpec(block, mine)] * len(got),
            out_specs=[pl.BlockSpec(block, place) for place in places],
        ),
        out_shape=[jax.ShapeDtypeStruct((n // len(places), rows, 128), jnp.bfloat16) for _ in places],
        compiler_params=PARAMS,
        cost_estimate=COST,
    )(blocks, g, wq.reshape(-1, 128, n_q), wkv.reshape(-1, 128, n_kv), *got)


def local(inputs, q_grad, key_value_share_gradient, q_weight, key_value_weight):
    q_columns = q_grad.shape[1]
    core = lax.axis_index("core")
    zhi = lax.axis_index("zhi")
    y = lax.axis_index(TOK)

    more = lax.ppermute(key_value_share_gradient, "core", SWAP)
    mine = own_rows(core.reshape(1), q_grad, key_value_share_gradient, more)
    far = lax.ppermute(mine, "zhi", SWAP)

    v = (y - core) % N_Y
    blocks_of = lambda at: jnp.stack(
        [second(at, jnp.where), third(second(at, jnp.where), jnp.where), at, third(at, jnp.where)]
    )
    keep_blocks = (blocks_of(v) + core) % N_Y
    give_blocks = (blocks_of(v + 1 - 2 * (v % 2)) + core) % N_Y
    zlo = lax.axis_index("zlo")
    heads = 2 * jnp.stack([zlo ^ 1, zlo ^ 3, zlo, zlo ^ 2])
    give_heads, keep_heads = heads + 1 - core, heads + core
    place = jnp.stack([lax.axis_index("x"), zhi])
    orders = (place, keep_blocks, give_blocks, give_heads, keep_heads)
    near = all_along_x(again(mine))
    far, orders = lax.optimization_barrier((far, orders))
    place, keep_blocks, give_blocks, give_heads, keep_heads = orders
    combined = in_order(place, near, all_along_x(far))

    def along_y(terms, pairs):
        return lax.ppermute(terms, (*TOK, "core"), pairs)

    given = give_terms(give_blocks, inputs, combined)
    first, for_input = lax.optimization_barrier((given[0], combined))
    got = [along_y(part, FIRST) for part in (first, *given[1:])]
    (give,) = input_terms(give_heads, for_input, q_weight, key_value_weight)
    core_got = lax.ppermute(give, "core", SWAP)
    give, input_keep = input_terms(keep_heads, for_input, q_weight, key_value_weight, core_got)
    input_got = lax.ppermute(give, "zlo", [(i, i ^ 1) for i in range(4)])

    after = input_keep
    parts = []
    at = 0
    for part in got:
        part, _ = lax.optimization_barrier((part, after))
        give, after = keep_terms(keep_blocks, inputs, combined, part, at)
        parts += [after, along_y(give, SECOND)]
        at += part.shape[-1]
    keep, give = add_terms(*parts)
    got = along_y(give, THIRD)

    input_keep, give = add_terms(input_keep, input_got)
    input_got = lax.ppermute(give, "zlo", [(i, i ^ 2) for i in range(4)])
    return last_sums(input_keep, input_got, keep, got, q_columns)


def solution(mesh):
    fine = Mesh(
        mesh.devices.reshape(4, 2, 4, 2, 4, 2), ("th", "tl", "zlo", "core", "x", "zhi")
    )
    return jax.shard_map(
        local,
        mesh=fine,
        in_specs=(
            P(TOK, WID),
            P((*TOK, *WID), HEAD),
            P((*TOK, *WID), HEAD),
            P(WID, HEAD),
            P(WID, HEAD),
        ),
        out_specs=(P(TOK, (*WID, *HEAD)), P((*WID, *TOK), HEAD), P((*WID, *TOK), HEAD)),
        check_vma=False,
    )
```

```python
import functools

import jax
import jax.numpy as jnp
from jax import lax
from jax.experimental import pallas as pl
from jax.experimental.pallas import tpu as pltpu
from jax.sharding import Mesh
from jax.sharding import PartitionSpec as P

SWAP = [(0, 1), (1, 0)]
WID = ("x", "zhi")
TOK = ("th", "tl")
HEAD = ("zlo", "core")
N_Y = 8
N_PAIRS = 4
VMEM_LIMIT = 32 * 2**20
COST = pl.CostEstimate(flops=1, bytes_accessed=1, transcendentals=0)
LONG = pl.CostEstimate(flops=5 * 10**10, bytes_accessed=1, transcendentals=0)


def inner(v, where):
    return where((v % 4 == 1) | (v % 4 == 2), True, False)


def second(v, where):
    return where(inner(v, where), (3 - v) % N_Y, (7 - v) % N_Y)


def third(v, where):
    return where(inner(v, where), (7 - v) % N_Y, (3 - v) % N_Y)


def select(condition, one, other):
    return one if condition else other


def swapped(partner):
    return [
        ((v + core) % N_Y * 2 + core, (partner(v) + core) % N_Y * 2 + core)
        for v in range(N_Y)
        for core in range(2)
    ]


FIRST = swapped(lambda v: v ^ 1)
SECOND = swapped(lambda v: second(v, select))
THIRD = swapped(lambda v: third(v, select))
PARTS = (640, 512)


VMEM = pl.BlockSpec(memory_space=pltpu.VMEM)
SMEM = pl.BlockSpec(memory_space=pltpu.SMEM)
PARAMS = pltpu.CompilerParams(vmem_limit_bytes=VMEM_LIMIT)


def own_body(core, q_hbm, share_hbm, more_ref, out_ref, share_ref, sems):
    n_q = q_hbm.shape[1]
    q_copy = pltpu.make_async_copy(q_hbm, out_ref.at[:, pl.ds(0, n_q)], sems.at[0])
    share_copy = pltpu.make_async_copy(share_hbm, share_ref, sems.at[1])
    q_copy.start()
    share_copy.start()
    share_copy.wait()
    columns = pl.ds(pl.multiple_of(core[0] * 128, 128), 128)
    kv = share_ref[:, columns].astype(jnp.float32) + more_ref[:, columns].astype(jnp.float32)
    out_ref[:, n_q:] = kv.astype(out_ref.dtype)
    q_copy.wait()


def own_rows(core, q, share, more):
    hbm = pl.BlockSpec(memory_space=pltpu.HBM)
    return pl.pallas_call(
        own_body,
        out_shape=jax.ShapeDtypeStruct((q.shape[0], q.shape[1] + 128), q.dtype),
        in_specs=[SMEM, hbm, hbm, VMEM],
        out_specs=VMEM,
        scratch_shapes=[pltpu.VMEM(share.shape, share.dtype), pltpu.SemaphoreType.DMA((2,))],
        compiler_params=PARAMS,
        cost_estimate=COST,
    )(core, q, share, more)


def again_body(rows_ref, out_ref):
    out_ref[...] = rows_ref[...]


def again(rows):
    return pl.pallas_call(
        again_body,
        out_shape=jax.ShapeDtypeStruct(rows.shape, rows.dtype),
        in_specs=[VMEM],
        out_specs=VMEM,
        compiler_params=PARAMS,
        cost_estimate=LONG,
    )(rows)


def x_swap(rows, partner):
    pairs = [
        (core * 4 + (u + core) % 4, core * 4 + (partner(u) + core) % 4)
        for core in range(2)
        for u in range(4)
    ]
    return lax.ppermute(rows, ("core", "x"), pairs)


def all_along_x(rows):
    pair = jnp.stack([rows, x_swap(rows, lambda u: u ^ 1)])
    return pair, x_swap(pair, lambda u: 3 - u)


def order_body(place, *refs):
    *pairs, out_ref = refs
    for i, pair in enumerate(pairs):
        zhi = place[4] if i < 2 else 1 - place[4]
        for j in range(2):
            out_ref[2 * place[2 * (i % 2) + j] + zhi] = pair[j]


def in_order(place, *pairs):
    _, rows, columns = pairs[0].shape
    return pl.pallas_call(
        order_body,
        out_shape=jax.ShapeDtypeStruct((2 * len(pairs), rows, columns), pairs[0].dtype),
        in_specs=[SMEM] + [VMEM] * len(pairs),
        out_specs=VMEM,
        compiler_params=PARAMS,
        cost_estimate=COST,
    )(place, *pairs).reshape(-1, columns)


def dot(left, right, dims):
    return lax.dot_general(left, right, ((dims[:1], dims[1:]), ((), ())), preferred_element_type=jnp.float32)


def give_body(blocks, x_ref, g_ref, *outs):
    for r in range(N_PAIRS):
        columns = x_ref[:, pl.ds(pl.multiple_of(blocks[r] * 128, 128), 128)]
        at = 0
        for out in outs:
            width = out.shape[-1]
            out[r] = dot(columns, g_ref[:, at : at + width], (0, 0)).astype(out.dtype)
            at += width


def give_terms(blocks, x, g):
    return pl.pallas_call(
        give_body,
        out_shape=[jax.ShapeDtypeStruct((N_PAIRS, 128, width), jnp.bfloat16) for width in PARTS],
        in_specs=[SMEM] + [VMEM] * 2,
        out_specs=[VMEM] * len(PARTS),
        compiler_params=PARAMS,
        cost_estimate=COST,
    )(blocks, x, g)


def keep_body(at, blocks, x_ref, g_ref, got_ref, give_ref, keep_ref):
    width = got_ref.shape[-1]
    for r in range(N_PAIRS):
        columns = x_ref[:, pl.ds(pl.multiple_of(blocks[r] * 128, 128), 128)]
        term = dot(columns, g_ref[:, at : at + width], (0, 0)) + got_ref[r].astype(jnp.float32)
        out = give_ref if r < 2 else keep_ref
        out[r % 2] = term.astype(out.dtype)


def keep_terms(blocks, x, g, got, at):
    return pl.pallas_call(
        functools.partial(keep_body, at),
        out_shape=[jax.ShapeDtypeStruct((2, *got.shape[1:]), jnp.bfloat16)] * 2,
        in_specs=[SMEM] + [VMEM] * 3,
        out_specs=[VMEM] * 2,
        compiler_params=PARAMS,
        cost_estimate=COST,
    )(blocks, x, g, got)


def add_body(*refs):
    *parts, keep_ref, give_ref = refs
    at = 0
    for kept, got in zip(parts[::2], parts[1::2]):
        width = kept.shape[-1]
        for r, out in enumerate((keep_ref, give_ref)):
            total = kept[r].astype(jnp.float32) + got[r].astype(jnp.float32)
            out[:, at : at + width] = total.astype(out.dtype)
        at += width


def add_terms(*parts):
    columns = sum(part.shape[-1] for part in parts[::2])
    return pl.pallas_call(
        add_body,
        out_shape=[jax.ShapeDtypeStruct((parts[0].shape[1], columns), jnp.bfloat16)] * 2,
        in_specs=[VMEM] * len(parts),
        out_specs=[VMEM] * 2,
        compiler_params=PARAMS,
        cost_estimate=COST,
    )(*parts)


def sum_body(input_kept, input_got, kept, got, input_out, q_ref, kv_ref):
    n_q = q_ref.shape[1]
    total = input_kept[...].astype(jnp.float32) + input_got[...].astype(jnp.float32)
    input_out[...] = total.astype(input_out.dtype)
    q_ref[...] = kept[:, :n_q].astype(jnp.float32) + got[:, :n_q].astype(jnp.float32)
    kv_ref[...] = kept[:, n_q:].astype(jnp.float32) + got[:, n_q:].astype(jnp.float32)


def last_sums(input_kept, input_got, kept, got, n_q):
    rows, columns = kept.shape
    outs = [
        jax.ShapeDtypeStruct(input_kept.shape, jnp.bfloat16),
        jax.ShapeDtypeStruct((rows, n_q), jnp.float32),
        jax.ShapeDtypeStruct((rows, columns - n_q), jnp.float32),
    ]
    block = lambda array: pl.BlockSpec(array.shape, lambda i: (0, 0))
    arrays = [input_kept, input_got, kept, got]
    return pl.pallas_call(
        sum_body,
        grid=(1,),
        out_shape=outs,
        in_specs=[block(array) for array in arrays],
        out_specs=[block(out) for out in outs],
        compiler_params=PARAMS,
        cost_estimate=COST,
    )(*arrays)


def input_body(blocks, g_ref, wq_ref, wkv_ref, *refs):
    n_q = wq_ref.shape[-1]
    term = dot(g_ref[:, :n_q], wq_ref[0], (1, 1))
    term = term + dot(g_ref[:, n_q:], wkv_ref[0], (1, 1))
    if len(refs) == 1:
        refs[0][0] = term.astype(jnp.bfloat16)
        return
    got_ref, *outs = refs
    term = (term + got_ref[0].astype(jnp.float32)).astype(jnp.bfloat16)
    for half, out in enumerate(outs):

        @pl.when(pl.program_id(0) // 2 == half)
        def _():
            out[0] = term


def input_terms(blocks, g, wq, wkv, *got):
    n_q, n_kv = wq.shape[1], wkv.shape[1]
    rows = g.shape[0]
    n = blocks.shape[0]
    pick = lambda r, blocks: (blocks[r], 0, 0)
    mine = lambda r, blocks: (r, 0, 0)
    block = (1, rows, 128)
    if got:
        places = [
            lambda r, blocks: (jnp.minimum(r, 1), 0, 0),
            lambda r, blocks: (jnp.maximum(r - 2, 0), 0, 0),
        ]
    else:
        places = [mine]
    return pl.pallas_call(
        input_body,
        grid_spec=pltpu.PrefetchScalarGridSpec(
            num_scalar_prefetch=1,
            grid=(n,),
            in_specs=[
                pl.BlockSpec(g.shape, lambda r, blocks: (0, 0)),
                pl.BlockSpec((1, 128, n_q), pick),
                pl.BlockSpec((1, 128, n_kv), pick),
            ]
            + [pl.BlockSpec(block, mine)] * len(got),
            out_specs=[pl.BlockSpec(block, place) for place in places],
        ),
        out_shape=[jax.ShapeDtypeStruct((n // len(places), rows, 128), jnp.bfloat16) for _ in places],
        compiler_params=PARAMS,
        cost_estimate=COST,
    )(blocks, g, wq.reshape(-1, 128, n_q), wkv.reshape(-1, 128, n_kv), *got)


def local(inputs, q_grad, key_value_share_gradient, q_weight, key_value_weight):
    q_columns = q_grad.shape[1]
    core = lax.axis_index("core")
    zhi = lax.axis_index("zhi")
    y = lax.axis_index(TOK)

    more = lax.ppermute(key_value_share_gradient, "core", SWAP)
    mine = own_rows(core.reshape(1), again(q_grad), key_value_share_gradient, more)
    far = lax.ppermute(mine, "zhi", SWAP)

    v = (y - core) % N_Y
    blocks_of = lambda at: jnp.stack(
        [second(at, jnp.where), third(second(at, jnp.where), jnp.where), at, third(at, jnp.where)]
    )
    keep_blocks = (blocks_of(v) + core) % N_Y
    give_blocks = (blocks_of(v + 1 - 2 * (v % 2)) + core) % N_Y
    zlo = lax.axis_index("zlo")
    heads = 2 * jnp.stack([zlo ^ 1, zlo ^ 3, zlo, zlo ^ 2])
    give_heads, keep_heads = heads + 1 - core, heads + core
    u = (lax.axis_index("x") - core) % 4
    place = jnp.stack([u, u ^ 1, 3 - u, (3 - u) ^ 1, zhi - core])
    place = (place + core) % 4
    orders = (place, keep_blocks, give_blocks, give_heads, keep_heads)
    near = all_along_x(again(mine))
    far, orders = lax.optimization_barrier((far, orders))
    place, keep_blocks, give_blocks, give_heads, keep_heads = orders
    combined = in_order(place, *near, *all_along_x(far))

    def along_y(terms, pairs):
        return lax.ppermute(terms, (*TOK, "core"), pairs)

    given = give_terms(give_blocks, inputs, combined)
    first, for_input = lax.optimization_barrier((given[0], combined))
    got = [along_y(part, FIRST) for part in (first, *given[1:])]
    (give,) = input_terms(give_heads, for_input, q_weight, key_value_weight)
    core_got = lax.ppermute(give, "core", SWAP)
    give, input_keep = input_terms(keep_heads, for_input, q_weight, key_value_weight, core_got)
    input_got = lax.ppermute(give, "zlo", [(i, i ^ 1) for i in range(4)])

    after = input_keep
    parts = []
    at = 0
    for part in got:
        part, _ = lax.optimization_barrier((part, after))
        give, after = keep_terms(keep_blocks, inputs, combined, part, at)
        parts += [after, along_y(give, SECOND)]
        at += part.shape[-1]
    keep, give = add_terms(*parts)
    got = along_y(give, THIRD)

    input_keep, give = add_terms(input_keep, input_got)
    input_got = lax.ppermute(give, "zlo", [(i, i ^ 2) for i in range(4)])
    return last_sums(input_keep, input_got, keep, got, q_columns)


def solution(mesh):
    fine = Mesh(
        mesh.devices.reshape(4, 2, 4, 2, 4, 2), ("th", "tl", "zlo", "core", "x", "zhi")
    )
    return jax.shard_map(
        local,
        mesh=fine,
        in_specs=(
            P(TOK, WID),
            P((*TOK, *WID), HEAD),
            P((*TOK, *WID), HEAD),
            P(WID, HEAD),
            P(WID, HEAD),
        ),
        out_specs=(P(TOK, (*WID, *HEAD)), P((*WID, *TOK), HEAD), P((*WID, *TOK), HEAD)),
        check_vma=False,
    )
```

```python
import functools

import jax
import jax.numpy as jnp
from jax import lax
from jax.experimental import pallas as pl
from jax.experimental.pallas import tpu as pltpu
from jax.sharding import Mesh
from jax.sharding import PartitionSpec as P

SWAP = [(0, 1), (1, 0)]
WID = ("x", "zhi")
TOK = ("th", "tl")
HEAD = ("zlo", "core")
N_Y = 8
N_PAIRS = 4
VMEM_LIMIT = 32 * 2**20
COST = pl.CostEstimate(flops=1, bytes_accessed=1, transcendentals=0)
LONG = pl.CostEstimate(flops=5 * 10**10, bytes_accessed=1, transcendentals=0)


def inner(v, where):
    return where((v % 4 == 1) | (v % 4 == 2), True, False)


def second(v, where):
    return where(inner(v, where), (3 - v) % N_Y, (7 - v) % N_Y)


def third(v, where):
    return where(inner(v, where), (7 - v) % N_Y, (3 - v) % N_Y)


def select(condition, one, other):
    return one if condition else other


def swapped(partner):
    return [
        ((v + core) % N_Y * 2 + core, (partner(v) + core) % N_Y * 2 + core)
        for v in range(N_Y)
        for core in range(2)
    ]


FIRST = swapped(lambda v: v ^ 1)
SECOND = swapped(lambda v: second(v, select))
THIRD = swapped(lambda v: third(v, select))
PARTS = (768, 384)


VMEM = pl.BlockSpec(memory_space=pltpu.VMEM)
SMEM = pl.BlockSpec(memory_space=pltpu.SMEM)
PARAMS = pltpu.CompilerParams(vmem_limit_bytes=VMEM_LIMIT)


def own_body(core, q_hbm, share_hbm, more_ref, out_ref, share_ref, sems):
    n_q = q_hbm.shape[1]
    q_copy = pltpu.make_async_copy(q_hbm, out_ref.at[:, pl.ds(0, n_q)], sems.at[0])
    share_copy = pltpu.make_async_copy(share_hbm, share_ref, sems.at[1])
    q_copy.start()
    share_copy.start()
    share_copy.wait()
    columns = pl.ds(pl.multiple_of(core[0] * 128, 128), 128)
    kv = share_ref[:, columns].astype(jnp.float32) + more_ref[:, columns].astype(jnp.float32)
    out_ref[:, n_q:] = kv.astype(out_ref.dtype)
    q_copy.wait()


def own_rows(core, q, share, more):
    hbm = pl.BlockSpec(memory_space=pltpu.HBM)
    return pl.pallas_call(
        own_body,
        out_shape=jax.ShapeDtypeStruct((q.shape[0], q.shape[1] + 128), q.dtype),
        in_specs=[SMEM, hbm, hbm, VMEM],
        out_specs=VMEM,
        scratch_shapes=[pltpu.VMEM(share.shape, share.dtype), pltpu.SemaphoreType.DMA((2,))],
        compiler_params=PARAMS,
        cost_estimate=COST,
    )(core, q, share, more)


def again_body(rows_ref, out_ref):
    out_ref[...] = rows_ref[...]


def again(rows):
    return pl.pallas_call(
        again_body,
        out_shape=jax.ShapeDtypeStruct(rows.shape, rows.dtype),
        in_specs=[VMEM],
        out_specs=VMEM,
        compiler_params=PARAMS,
        cost_estimate=LONG,
    )(rows)


def x_swap(rows, partner):
    pairs = [
        (core * 4 + (u + core) % 4, core * 4 + (partner(u) + core) % 4)
        for core in range(2)
        for u in range(4)
    ]
    return lax.ppermute(rows, ("core", "x"), pairs)


def all_along_x(rows):
    pair = jnp.stack([rows, x_swap(rows, lambda u: u ^ 1)])
    return pair, x_swap(pair, lambda u: 3 - u)


def order_body(place, *refs):
    *pairs, out_ref = refs
    for i, pair in enumerate(pairs):
        zhi = place[4] if i < 2 else 1 - place[4]
        for j in range(2):
            out_ref[2 * place[2 * (i % 2) + j] + zhi] = pair[j]


def in_order(place, *pairs):
    _, rows, columns = pairs[0].shape
    return pl.pallas_call(
        order_body,
        out_shape=jax.ShapeDtypeStruct((2 * len(pairs), rows, columns), pairs[0].dtype),
        in_specs=[SMEM] + [VMEM] * len(pairs),
        out_specs=VMEM,
        compiler_params=PARAMS,
        cost_estimate=COST,
    )(place, *pairs).reshape(-1, columns)


def dot(left, right, dims):
    return lax.dot_general(left, right, ((dims[:1], dims[1:]), ((), ())), preferred_element_type=jnp.float32)


def give_body(blocks, x_ref, g_ref, *outs):
    for r in range(N_PAIRS):
        columns = x_ref[:, pl.ds(pl.multiple_of(blocks[r] * 128, 128), 128)]
        at = 0
        for out in outs:
            width = out.shape[-1]
            out[r] = dot(columns, g_ref[:, at : at + width], (0, 0)).astype(out.dtype)
            at += width


def give_terms(blocks, x, g):
    return pl.pallas_call(
        give_body,
        out_shape=[jax.ShapeDtypeStruct((N_PAIRS, 128, width), jnp.bfloat16) for width in PARTS],
        in_specs=[SMEM] + [VMEM] * 2,
        out_specs=[VMEM] * len(PARTS),
        compiler_params=PARAMS,
        cost_estimate=COST,
    )(blocks, x, g)


def keep_body(at, blocks, x_ref, g_ref, got_ref, give_ref, keep_ref):
    width = got_ref.shape[-1]
    for r in range(N_PAIRS):
        columns = x_ref[:, pl.ds(pl.multiple_of(blocks[r] * 128, 128), 128)]
        term = dot(columns, g_ref[:, at : at + width], (0, 0)) + got_ref[r].astype(jnp.float32)
        out = give_ref if r < 2 else keep_ref
        out[r % 2] = term.astype(out.dtype)


def keep_terms(blocks, x, g, got, at):
    return pl.pallas_call(
        functools.partial(keep_body, at),
        out_shape=[jax.ShapeDtypeStruct((2, *got.shape[1:]), jnp.bfloat16)] * 2,
        in_specs=[SMEM] + [VMEM] * 3,
        out_specs=[VMEM] * 2,
        compiler_params=PARAMS,
        cost_estimate=COST,
    )(blocks, x, g, got)


def add_body(*refs):
    *parts, keep_ref, give_ref = refs
    at = 0
    for kept, got in zip(parts[::2], parts[1::2]):
        width = kept.shape[-1]
        for r, out in enumerate((keep_ref, give_ref)):
            total = kept[r].astype(jnp.float32) + got[r].astype(jnp.float32)
            out[:, at : at + width] = total.astype(out.dtype)
        at += width


def add_terms(*parts):
    columns = sum(part.shape[-1] for part in parts[::2])
    return pl.pallas_call(
        add_body,
        out_shape=[jax.ShapeDtypeStruct((parts[0].shape[1], columns), jnp.bfloat16)] * 2,
        in_specs=[VMEM] * len(parts),
        out_specs=[VMEM] * 2,
        compiler_params=PARAMS,
        cost_estimate=COST,
    )(*parts)


def sum_body(input_kept, input_got, kept, got, input_out, q_ref, kv_ref):
    n_q = q_ref.shape[1]
    total = input_kept[...].astype(jnp.float32) + input_got[...].astype(jnp.float32)
    input_out[...] = total.astype(input_out.dtype)
    q_ref[...] = kept[:, :n_q].astype(jnp.float32) + got[:, :n_q].astype(jnp.float32)
    kv_ref[...] = kept[:, n_q:].astype(jnp.float32) + got[:, n_q:].astype(jnp.float32)


def last_sums(input_kept, input_got, kept, got, n_q):
    rows, columns = kept.shape
    outs = [
        jax.ShapeDtypeStruct(input_kept.shape, jnp.bfloat16),
        jax.ShapeDtypeStruct((rows, n_q), jnp.float32),
        jax.ShapeDtypeStruct((rows, columns - n_q), jnp.float32),
    ]
    block = lambda array: pl.BlockSpec(array.shape, lambda i: (0, 0))
    arrays = [input_kept, input_got, kept, got]
    return pl.pallas_call(
        sum_body,
        grid=(1,),
        out_shape=outs,
        in_specs=[block(array) for array in arrays],
        out_specs=[block(out) for out in outs],
        compiler_params=PARAMS,
        cost_estimate=COST,
    )(*arrays)


def input_body(blocks, g_ref, wq_one, wq_two, wkv_one, wkv_two, *refs):
    n_q = wq_one.shape[-1]
    wq = jnp.concatenate([wq_one[0], wq_two[0]])
    wkv = jnp.concatenate([wkv_one[0], wkv_two[0]])
    term = dot(g_ref[:, :n_q], wq, (1, 1)) + dot(g_ref[:, n_q:], wkv, (1, 1))
    pair = [term[:, :128], term[:, 128:]]
    if len(refs) == 1:
        for i in range(2):
            refs[0][i] = pair[i].astype(jnp.bfloat16)
        return
    got_ref, *outs = refs
    for half, out in enumerate(outs):

        @pl.when(pl.program_id(0) == half)
        def _():
            for i in range(2):
                out[i] = (pair[i] + got_ref[i].astype(jnp.float32)).astype(jnp.bfloat16)


def input_terms(blocks, g, wq, wkv, *got):
    n_q, n_kv = wq.shape[1], wkv.shape[1]
    rows = g.shape[0]
    n = blocks.shape[0]
    one = lambda r, blocks: (blocks[2 * r], 0, 0)
    two = lambda r, blocks: (blocks[2 * r + 1], 0, 0)
    mine = lambda r, blocks: (r, 0, 0)
    fixed = lambda r, blocks: (0, 0, 0)
    block = (2, rows, 128)
    places = [fixed, fixed] if got else [mine]
    wq, wkv = wq.reshape(-1, 128, n_q), wkv.reshape(-1, 128, n_kv)
    return pl.pallas_call(
        input_body,
        grid_spec=pltpu.PrefetchScalarGridSpec(
            num_scalar_prefetch=1,
            grid=(n // 2,),
            in_specs=[
                pl.BlockSpec(g.shape, lambda r, blocks: (0, 0)),
                pl.BlockSpec((1, 128, n_q), one),
                pl.BlockSpec((1, 128, n_q), two),
                pl.BlockSpec((1, 128, n_kv), one),
                pl.BlockSpec((1, 128, n_kv), two),
            ]
            + [pl.BlockSpec(block, mine)] * len(got),
            out_specs=[pl.BlockSpec(block, place) for place in places],
        ),
        out_shape=[jax.ShapeDtypeStruct((n // len(places), rows, 128), jnp.bfloat16) for _ in places],
        compiler_params=PARAMS,
        cost_estimate=COST,
    )(blocks, g, wq, wq, wkv, wkv, *got)


def local(inputs, q_grad, key_value_share_gradient, q_weight, key_value_weight):
    q_columns = q_grad.shape[1]
    core = lax.axis_index("core")
    zhi = lax.axis_index("zhi")
    y = lax.axis_index(TOK)

    more = lax.ppermute(key_value_share_gradient, "core", SWAP)
    mine = own_rows(core.reshape(1), again(q_grad), key_value_share_gradient, more)
    far = lax.ppermute(mine, "zhi", SWAP)

    v = (y - core) % N_Y
    blocks_of = lambda at: jnp.stack(
        [second(at, jnp.where), third(second(at, jnp.where), jnp.where), at, third(at, jnp.where)]
    )
    keep_blocks = (blocks_of(v) + core) % N_Y
    give_blocks = (blocks_of(v + 1 - 2 * (v % 2)) + core) % N_Y
    zlo = lax.axis_index("zlo")
    heads = 2 * jnp.stack([zlo ^ 1, zlo ^ 3, zlo, zlo ^ 2])
    give_heads, keep_heads = heads + 1 - core, heads + core
    u = (lax.axis_index("x") - core) % 4
    place = jnp.stack([u, u ^ 1, 3 - u, (3 - u) ^ 1, zhi - core])
    place = (place + core) % 4
    orders = (place, keep_blocks, give_blocks, give_heads, keep_heads)
    near = all_along_x(again(mine))
    far, orders = lax.optimization_barrier((far, orders))
    place, keep_blocks, give_blocks, give_heads, keep_heads = orders
    combined = in_order(place, *near, *all_along_x(far))

    def along_y(terms, pairs):
        return lax.ppermute(terms, (*TOK, "core"), pairs)

    given = give_terms(give_blocks, inputs, combined)
    first, for_input = lax.optimization_barrier((given[0], combined))
    got = [along_y(part, FIRST) for part in (first, *given[1:])]
    (give,) = input_terms(give_heads, for_input, q_weight, key_value_weight)
    core_got = lax.ppermute(give, "core", SWAP)
    give, input_keep = input_terms(keep_heads, for_input, q_weight, key_value_weight, core_got)
    input_got = lax.ppermute(give, "zlo", [(i, i ^ 1) for i in range(4)])

    after = input_keep
    parts = []
    at = 0
    for part in got:
        part, _ = lax.optimization_barrier((part, after))
        give, after = keep_terms(keep_blocks, inputs, combined, part, at)
        parts += [after, along_y(give, SECOND)]
        at += part.shape[-1]
    keep, give = add_terms(*parts)
    got = along_y(give, THIRD)

    input_keep, give = add_terms(input_keep, input_got)
    input_got = lax.ppermute(give, "zlo", [(i, i ^ 2) for i in range(4)])
    return last_sums(input_keep, input_got, keep, got, q_columns)


def solution(mesh):
    fine = Mesh(
        mesh.devices.reshape(4, 2, 4, 2, 4, 2), ("th", "tl", "zlo", "core", "x", "zhi")
    )
    return jax.shard_map(
        local,
        mesh=fine,
        in_specs=(
            P(TOK, WID),
            P((*TOK, *WID), HEAD),
            P((*TOK, *WID), HEAD),
            P(WID, HEAD),
            P(WID, HEAD),
        ),
        out_specs=(P(TOK, (*WID, *HEAD)), P((*WID, *TOK), HEAD), P((*WID, *TOK), HEAD)),
        check_vma=False,
    )
```

```python
import functools

import jax
import jax.numpy as jnp
from jax import lax
from jax.experimental import pallas as pl
from jax.experimental.pallas import tpu as pltpu
from jax.sharding import Mesh
from jax.sharding import PartitionSpec as P

SWAP = [(0, 1), (1, 0)]
WID = ("x", "zhi")
TOK = ("th", "tl")
HEAD = ("zlo", "core")
N_Y = 8
N_PAIRS = 4
VMEM_LIMIT = 32 * 2**20
COST = pl.CostEstimate(flops=1, bytes_accessed=1, transcendentals=0)
LONG = pl.CostEstimate(flops=5 * 10**10, bytes_accessed=1, transcendentals=0)


def inner(v, where):
    return where((v % 4 == 1) | (v % 4 == 2), True, False)


def second(v, where):
    return where(inner(v, where), (3 - v) % N_Y, (7 - v) % N_Y)


def third(v, where):
    return where(inner(v, where), (7 - v) % N_Y, (3 - v) % N_Y)


def select(condition, one, other):
    return one if condition else other


def swapped(partner):
    return [
        ((v + core) % N_Y * 2 + core, (partner(v) + core) % N_Y * 2 + core)
        for v in range(N_Y)
        for core in range(2)
    ]


FIRST = swapped(lambda v: v ^ 1)
SECOND = swapped(lambda v: second(v, select))
THIRD = swapped(lambda v: third(v, select))
PARTS = (768, 384)


VMEM = pl.BlockSpec(memory_space=pltpu.VMEM)
SMEM = pl.BlockSpec(memory_space=pltpu.SMEM)
PARAMS = pltpu.CompilerParams(vmem_limit_bytes=VMEM_LIMIT)


def own_body(core, q_hbm, share_hbm, more_ref, out_ref, share_ref, sems):
    n_q = q_hbm.shape[1]
    q_copy = pltpu.make_async_copy(q_hbm, out_ref.at[:, pl.ds(0, n_q)], sems.at[0])
    share_copy = pltpu.make_async_copy(share_hbm, share_ref, sems.at[1])
    q_copy.start()
    share_copy.start()
    share_copy.wait()
    columns = pl.ds(pl.multiple_of(core[0] * 128, 128), 128)
    kv = share_ref[:, columns].astype(jnp.float32) + more_ref[:, columns].astype(jnp.float32)
    out_ref[:, n_q:] = kv.astype(out_ref.dtype)
    q_copy.wait()


def own_rows(core, q, share, more):
    hbm = pl.BlockSpec(memory_space=pltpu.HBM)
    return pl.pallas_call(
        own_body,
        out_shape=jax.ShapeDtypeStruct((q.shape[0], q.shape[1] + 128), q.dtype),
        in_specs=[SMEM, hbm, hbm, VMEM],
        out_specs=VMEM,
        scratch_shapes=[pltpu.VMEM(share.shape, share.dtype), pltpu.SemaphoreType.DMA((2,))],
        compiler_params=PARAMS,
        cost_estimate=COST,
    )(core, q, share, more)


def again_body(rows_ref, out_ref):
    out_ref[...] = rows_ref[...]


def again(rows):
    return pl.pallas_call(
        again_body,
        out_shape=jax.ShapeDtypeStruct(rows.shape, rows.dtype),
        in_specs=[VMEM],
        out_specs=VMEM,
        compiler_params=PARAMS,
        cost_estimate=LONG,
    )(rows)


def x_swap(rows, partner):
    pairs = [
        (core * 4 + (u + core) % 4, core * 4 + (partner(u) + core) % 4)
        for core in range(2)
        for u in range(4)
    ]
    return lax.ppermute(rows, ("core", "x"), pairs)


def first_pair(rows):
    return jnp.stack([rows, x_swap(rows, lambda u: u ^ 1)])


def second_pair(pair):
    return x_swap(pair, lambda u: 3 - u)


def order_body(at, place, *refs):
    *pairs, out_ref = refs
    width = out_ref.shape[-1]
    for i, pair in enumerate(pairs):
        zhi = place[4] if i < 2 else 1 - place[4]
        for j in range(2):
            rows = pair[j] if pair.shape[-1] == width else pair[j, :, at : at + width]
            out_ref[2 * place[2 * (i % 2) + j] + zhi] = rows


def in_order(at, place, *pairs):
    _, rows, width = pairs[-1].shape
    return pl.pallas_call(
        functools.partial(order_body, at),
        out_shape=jax.ShapeDtypeStruct((2 * len(pairs), rows, width), pairs[0].dtype),
        in_specs=[SMEM] + [VMEM] * len(pairs),
        out_specs=VMEM,
        compiler_params=PARAMS,
        cost_estimate=COST,
    )(place, *pairs).reshape(-1, width)


def dot(left, right, dims):
    return lax.dot_general(left, right, ((dims[:1], dims[1:]), ((), ())), preferred_element_type=jnp.float32)


def give_body(blocks, x_ref, g_ref, out_ref):
    for r in range(N_PAIRS):
        columns = x_ref[:, pl.ds(pl.multiple_of(blocks[r] * 128, 128), 128)]
        out_ref[r] = dot(columns, g_ref[...], (0, 0)).astype(out_ref.dtype)


def give_terms(blocks, x, g):
    return pl.pallas_call(
        give_body,
        out_shape=jax.ShapeDtypeStruct((N_PAIRS, 128, g.shape[1]), jnp.bfloat16),
        in_specs=[SMEM] + [VMEM] * 2,
        out_specs=VMEM,
        compiler_params=PARAMS,
        cost_estimate=COST,
    )(blocks, x, g)


def keep_body(blocks, x_ref, g_ref, got_ref, give_ref, keep_ref):
    for r in range(N_PAIRS):
        columns = x_ref[:, pl.ds(pl.multiple_of(blocks[r] * 128, 128), 128)]
        term = dot(columns, g_ref[...], (0, 0)) + got_ref[r].astype(jnp.float32)
        out = give_ref if r < 2 else keep_ref
        out[r % 2] = term.astype(out.dtype)


def keep_terms(blocks, x, g, got):
    return pl.pallas_call(
        keep_body,
        out_shape=[jax.ShapeDtypeStruct((2, *got.shape[1:]), jnp.bfloat16)] * 2,
        in_specs=[SMEM] + [VMEM] * 3,
        out_specs=[VMEM] * 2,
        compiler_params=PARAMS,
        cost_estimate=COST,
    )(blocks, x, g, got)


def add_body(*refs):
    *parts, keep_ref, give_ref = refs
    at = 0
    for kept, got in zip(parts[::2], parts[1::2]):
        width = kept.shape[-1]
        for r, out in enumerate((keep_ref, give_ref)):
            total = kept[r].astype(jnp.float32) + got[r].astype(jnp.float32)
            out[:, at : at + width] = total.astype(out.dtype)
        at += width


def add_terms(*parts):
    columns = sum(part.shape[-1] for part in parts[::2])
    return pl.pallas_call(
        add_body,
        out_shape=[jax.ShapeDtypeStruct((parts[0].shape[1], columns), jnp.bfloat16)] * 2,
        in_specs=[VMEM] * len(parts),
        out_specs=[VMEM] * 2,
        compiler_params=PARAMS,
        cost_estimate=COST,
    )(*parts)


def sum_body(input_kept, input_got, kept, got, input_out, q_ref, kv_ref):
    n_q = q_ref.shape[1]
    total = input_kept[...].astype(jnp.float32) + input_got[...].astype(jnp.float32)
    input_out[...] = total.astype(input_out.dtype)
    q_ref[...] = kept[:, :n_q].astype(jnp.float32) + got[:, :n_q].astype(jnp.float32)
    kv_ref[...] = kept[:, n_q:].astype(jnp.float32) + got[:, n_q:].astype(jnp.float32)


def last_sums(input_kept, input_got, kept, got, n_q):
    rows, columns = kept.shape
    outs = [
        jax.ShapeDtypeStruct(input_kept.shape, jnp.bfloat16),
        jax.ShapeDtypeStruct((rows, n_q), jnp.float32),
        jax.ShapeDtypeStruct((rows, columns - n_q), jnp.float32),
    ]
    block = lambda array: pl.BlockSpec(array.shape, lambda i: (0, 0))
    arrays = [input_kept, input_got, kept, got]
    return pl.pallas_call(
        sum_body,
        grid=(1,),
        out_shape=outs,
        in_specs=[block(array) for array in arrays],
        out_specs=[block(out) for out in outs],
        compiler_params=PARAMS,
        cost_estimate=COST,
    )(*arrays)


def input_body(blocks, one_ref, two_ref, wq_one, wq_two, wkv_one, wkv_two, *refs):
    n_q = wq_one.shape[-1]
    wq = jnp.concatenate([wq_one[0], wq_two[0]])
    wkv = jnp.concatenate([wkv_one[0], wkv_two[0]])
    split = one_ref.shape[1]
    term = dot(one_ref[...], wq[:, :split], (1, 1)) + dot(two_ref[:, : n_q - split], wq[:, split:], (1, 1))
    term = term + dot(two_ref[:, n_q - split :], wkv, (1, 1))
    pair = [term[:, :128], term[:, 128:]]
    if len(refs) == 1:
        for i in range(2):
            refs[0][i] = pair[i].astype(jnp.bfloat16)
        return
    got_ref, *outs = refs
    for half, out in enumerate(outs):

        @pl.when(pl.program_id(0) == half)
        def _():
            for i in range(2):
                out[i] = (pair[i] + got_ref[i].astype(jnp.float32)).astype(jnp.bfloat16)


def input_terms(blocks, one_part, two_part, wq, wkv, *got):
    n_q, n_kv = wq.shape[1], wkv.shape[1]
    rows = one_part.shape[0]
    n = blocks.shape[0]
    one = lambda r, blocks: (blocks[2 * r], 0, 0)
    two = lambda r, blocks: (blocks[2 * r + 1], 0, 0)
    mine = lambda r, blocks: (r, 0, 0)
    fixed = lambda r, blocks: (0, 0, 0)
    block = (2, rows, 128)
    places = [fixed, fixed] if got else [mine]
    wq, wkv = wq.reshape(-1, 128, n_q), wkv.reshape(-1, 128, n_kv)
    return pl.pallas_call(
        input_body,
        grid_spec=pltpu.PrefetchScalarGridSpec(
            num_scalar_prefetch=1,
            grid=(n // 2,),
            in_specs=[
                pl.BlockSpec(one_part.shape, lambda r, blocks: (0, 0)),
                pl.BlockSpec(two_part.shape, lambda r, blocks: (0, 0)),
                pl.BlockSpec((1, 128, n_q), one),
                pl.BlockSpec((1, 128, n_q), two),
                pl.BlockSpec((1, 128, n_kv), one),
                pl.BlockSpec((1, 128, n_kv), two),
            ]
            + [pl.BlockSpec(block, mine)] * len(got),
            out_specs=[pl.BlockSpec(block, place) for place in places],
        ),
        out_shape=[jax.ShapeDtypeStruct((n // len(places), rows, 128), jnp.bfloat16) for _ in places],
        compiler_params=PARAMS,
        cost_estimate=COST,
    )(blocks, one_part, two_part, wq, wq, wkv, wkv, *got)


def local(inputs, q_grad, key_value_share_gradient, q_weight, key_value_weight):
    q_columns = q_grad.shape[1]
    core = lax.axis_index("core")
    zhi = lax.axis_index("zhi")
    y = lax.axis_index(TOK)

    more = lax.ppermute(key_value_share_gradient, "core", SWAP)
    mine = own_rows(core.reshape(1), again(q_grad), key_value_share_gradient, more)
    far = lax.ppermute(mine, "zhi", SWAP)

    v = (y - core) % N_Y
    blocks_of = lambda at: jnp.stack(
        [second(at, jnp.where), third(second(at, jnp.where), jnp.where), at, third(at, jnp.where)]
    )
    keep_blocks = (blocks_of(v) + core) % N_Y
    give_blocks = (blocks_of(v + 1 - 2 * (v % 2)) + core) % N_Y
    zlo = lax.axis_index("zlo")
    heads = 2 * jnp.stack([zlo ^ 1, zlo ^ 3, zlo, zlo ^ 2])
    give_heads, keep_heads = heads + 1 - core, heads + core
    u = (lax.axis_index("x") - core) % 4
    place = jnp.stack([u, u ^ 1, 3 - u, (3 - u) ^ 1, zhi - core])
    place = (place + core) % 4
    orders = (place, keep_blocks, give_blocks, give_heads, keep_heads)
    near = first_pair(again(mine))
    near = [near, second_pair(near)]
    far, orders = lax.optimization_barrier((far, orders))
    place, keep_blocks, give_blocks, give_heads, keep_heads = orders
    pair = first_pair(far)
    others = []
    at = 0
    for width in PARTS:
        others.append(second_pair(pair[:, :, at : at + width]))
        at += width

    def along_y(terms, pairs):
        return lax.ppermute(terms, (*TOK, "core"), pairs)

    combined = [in_order(0, place, *near, pair, others[0])]
    given = [give_terms(give_blocks, inputs, combined[0])]
    given[0], others[1] = lax.optimization_barrier((given[0], others[1]))
    combined.append(in_order(PARTS[0], place, *near, pair, others[1]))
    given.append(give_terms(give_blocks, inputs, combined[1]))
    got = [along_y(part, FIRST) for part in given]
    (give,) = input_terms(give_heads, *combined, q_weight, key_value_weight)
    core_got = lax.ppermute(give, "core", SWAP)
    give, input_keep = input_terms(keep_heads, *combined, q_weight, key_value_weight, core_got)
    input_got = lax.ppermute(give, "zlo", [(i, i ^ 1) for i in range(4)])

    after = input_keep
    parts = []
    for columns, part in zip(combined, got):
        part, _ = lax.optimization_barrier((part, after))
        give, after = keep_terms(keep_blocks, inputs, columns, part)
        parts += [after, along_y(give, SECOND)]
    keep, give = add_terms(*parts)
    got = along_y(give, THIRD)

    input_keep, give = add_terms(input_keep, input_got)
    input_got = lax.ppermute(give, "zlo", [(i, i ^ 2) for i in range(4)])
    return last_sums(input_keep, input_got, keep, got, q_columns)


def solution(mesh):
    fine = Mesh(
        mesh.devices.reshape(4, 2, 4, 2, 4, 2), ("th", "tl", "zlo", "core", "x", "zhi")
    )
    return jax.shard_map(
        local,
        mesh=fine,
        in_specs=(
            P(TOK, WID),
            P((*TOK, *WID), HEAD),
            P((*TOK, *WID), HEAD),
            P(WID, HEAD),
            P(WID, HEAD),
        ),
        out_specs=(P(TOK, (*WID, *HEAD)), P((*WID, *TOK), HEAD), P((*WID, *TOK), HEAD)),
        check_vma=False,
    )
```

```python
import functools

import jax
import jax.numpy as jnp
from jax import lax
from jax.experimental import pallas as pl
from jax.experimental.pallas import tpu as pltpu
from jax.sharding import Mesh
from jax.sharding import PartitionSpec as P

SWAP = [(0, 1), (1, 0)]
WID = ("x", "zhi")
TOK = ("th", "tl")
HEAD = ("zlo", "core")
N_Y = 8
N_PAIRS = 4
VMEM_LIMIT = 32 * 2**20
COST = pl.CostEstimate(flops=1, bytes_accessed=1, transcendentals=0)
LONG = pl.CostEstimate(flops=5 * 10**10, bytes_accessed=1, transcendentals=0)


def inner(v, where):
    return where((v % 4 == 1) | (v % 4 == 2), True, False)


def second(v, where):
    return where(inner(v, where), (3 - v) % N_Y, (7 - v) % N_Y)


def third(v, where):
    return where(inner(v, where), (7 - v) % N_Y, (3 - v) % N_Y)


def select(condition, one, other):
    return one if condition else other


def swapped(partner):
    return [
        ((v + core) % N_Y * 2 + core, (partner(v) + core) % N_Y * 2 + core)
        for v in range(N_Y)
        for core in range(2)
    ]


FIRST = swapped(lambda v: v ^ 1)
SECOND = swapped(lambda v: second(v, select))
THIRD = swapped(lambda v: third(v, select))
PARTS = (768, 384)


VMEM = pl.BlockSpec(memory_space=pltpu.VMEM)
SMEM = pl.BlockSpec(memory_space=pltpu.SMEM)
PARAMS = pltpu.CompilerParams(vmem_limit_bytes=VMEM_LIMIT)


def own_body(core, q_hbm, share_hbm, more_ref, out_ref, share_ref, sems):
    n_q = q_hbm.shape[1]
    q_copy = pltpu.make_async_copy(q_hbm, out_ref.at[:, pl.ds(0, n_q)], sems.at[0])
    share_copy = pltpu.make_async_copy(share_hbm, share_ref, sems.at[1])
    q_copy.start()
    share_copy.start()
    share_copy.wait()
    columns = pl.ds(pl.multiple_of(core[0] * 128, 128), 128)
    kv = share_ref[:, columns].astype(jnp.float32) + more_ref[:, columns].astype(jnp.float32)
    out_ref[:, n_q:] = kv.astype(out_ref.dtype)
    q_copy.wait()


def own_rows(core, q, share, more):
    hbm = pl.BlockSpec(memory_space=pltpu.HBM)
    return pl.pallas_call(
        own_body,
        out_shape=jax.ShapeDtypeStruct((q.shape[0], q.shape[1] + 128), q.dtype),
        in_specs=[SMEM, hbm, hbm, VMEM],
        out_specs=VMEM,
        scratch_shapes=[pltpu.VMEM(share.shape, share.dtype), pltpu.SemaphoreType.DMA((2,))],
        compiler_params=PARAMS,
        cost_estimate=COST,
    )(core, q, share, more)


def again_body(rows_ref, out_ref):
    out_ref[...] = rows_ref[...]


def again(rows):
    return pl.pallas_call(
        again_body,
        out_shape=jax.ShapeDtypeStruct(rows.shape, rows.dtype),
        in_specs=[VMEM],
        out_specs=VMEM,
        compiler_params=PARAMS,
        cost_estimate=LONG,
    )(rows)


def x_swap(rows, partner):
    pairs = [
        (core * 4 + (u + core) % 4, core * 4 + (partner(u) + core) % 4)
        for core in range(2)
        for u in range(4)
    ]
    return lax.ppermute(rows, ("core", "x"), pairs)


def all_along_x(rows):
    pair = jnp.stack([rows, x_swap(rows, lambda u: u ^ 1)])
    return pair, x_swap(pair, lambda u: 3 - u)


def order_body(place, *refs):
    *pairs, out_ref = refs
    for i, pair in enumerate(pairs):
        zhi = place[4] if i < 2 else 1 - place[4]
        for j in range(2):
            out_ref[2 * place[2 * (i % 2) + j] + zhi] = pair[j]


def in_order(place, *pairs):
    _, rows, columns = pairs[0].shape
    return pl.pallas_call(
        order_body,
        out_shape=jax.ShapeDtypeStruct((2 * len(pairs), rows, columns), pairs[0].dtype),
        in_specs=[SMEM] + [VMEM] * len(pairs),
        out_specs=VMEM,
        compiler_params=PARAMS,
        cost_estimate=COST,
    )(place, *pairs).reshape(-1, columns)


def dot(left, right, dims):
    return lax.dot_general(left, right, ((dims[:1], dims[1:]), ((), ())), preferred_element_type=jnp.float32)


def joined(blocks, x_ref):
    return jnp.concatenate(
        [x_ref[:, pl.ds(pl.multiple_of(blocks[r] * 128, 128), 128)] for r in range(N_PAIRS)], axis=1
    )


def give_body(blocks, x_ref, g_ref, *outs):
    columns = joined(blocks, x_ref)
    at = 0
    for out in outs:
        width = out.shape[-1]
        term = dot(columns, g_ref[:, at : at + width], (0, 0))
        for r in range(N_PAIRS):
            out[r] = term[r * 128 : (r + 1) * 128].astype(out.dtype)
        at += width


def give_terms(blocks, x, g):
    return pl.pallas_call(
        give_body,
        out_shape=[jax.ShapeDtypeStruct((N_PAIRS, 128, width), jnp.bfloat16) for width in PARTS],
        in_specs=[SMEM] + [VMEM] * 2,
        out_specs=[VMEM] * len(PARTS),
        compiler_params=PARAMS,
        cost_estimate=COST,
    )(blocks, x, g)


def keep_body(at, blocks, x_ref, g_ref, got_ref, give_ref, keep_ref):
    width = got_ref.shape[-1]
    term = dot(joined(blocks, x_ref), g_ref[:, at : at + width], (0, 0))
    for r in range(N_PAIRS):
        total = term[r * 128 : (r + 1) * 128] + got_ref[r].astype(jnp.float32)
        out = give_ref if r < 2 else keep_ref
        out[r % 2] = total.astype(out.dtype)


def keep_terms(blocks, x, g, got, at):
    return pl.pallas_call(
        functools.partial(keep_body, at),
        out_shape=[jax.ShapeDtypeStruct((2, *got.shape[1:]), jnp.bfloat16)] * 2,
        in_specs=[SMEM] + [VMEM] * 3,
        out_specs=[VMEM] * 2,
        compiler_params=PARAMS,
        cost_estimate=COST,
    )(blocks, x, g, got)


def add_body(*refs):
    *parts, keep_ref, give_ref = refs
    at = 0
    for kept, got in zip(parts[::2], parts[1::2]):
        width = kept.shape[-1]
        for r, out in enumerate((keep_ref, give_ref)):
            total = kept[r].astype(jnp.float32) + got[r].astype(jnp.float32)
            out[:, at : at + width] = total.astype(out.dtype)
        at += width


def add_terms(*parts):
    columns = sum(part.shape[-1] for part in parts[::2])
    return pl.pallas_call(
        add_body,
        out_shape=[jax.ShapeDtypeStruct((parts[0].shape[1], columns), jnp.bfloat16)] * 2,
        in_specs=[VMEM] * len(parts),
        out_specs=[VMEM] * 2,
        compiler_params=PARAMS,
        cost_estimate=COST,
    )(*parts)


def sum_body(input_kept, input_got, kept, got, input_out, q_ref, kv_ref):
    n_q = q_ref.shape[1]
    total = input_kept[...].astype(jnp.float32) + input_got[...].astype(jnp.float32)
    input_out[...] = total.astype(input_out.dtype)
    q_ref[...] = kept[:, :n_q].astype(jnp.float32) + got[:, :n_q].astype(jnp.float32)
    kv_ref[...] = kept[:, n_q:].astype(jnp.float32) + got[:, n_q:].astype(jnp.float32)


def last_sums(input_kept, input_got, kept, got, n_q):
    rows, columns = kept.shape
    outs = [
        jax.ShapeDtypeStruct(input_kept.shape, jnp.bfloat16),
        jax.ShapeDtypeStruct((rows, n_q), jnp.float32),
        jax.ShapeDtypeStruct((rows, columns - n_q), jnp.float32),
    ]
    block = lambda array: pl.BlockSpec(array.shape, lambda i: (0, 0))
    arrays = [input_kept, input_got, kept, got]
    return pl.pallas_call(
        sum_body,
        grid=(1,),
        out_shape=outs,
        in_specs=[block(array) for array in arrays],
        out_specs=[block(out) for out in outs],
        compiler_params=PARAMS,
        cost_estimate=COST,
    )(*arrays)


def input_body(blocks, g_ref, wq_one, wq_two, wkv_one, wkv_two, *refs):
    n_q = wq_one.shape[-1]
    wq = jnp.concatenate([wq_one[0], wq_two[0]])
    wkv = jnp.concatenate([wkv_one[0], wkv_two[0]])
    term = dot(g_ref[:, :n_q], wq, (1, 1)) + dot(g_ref[:, n_q:], wkv, (1, 1))
    pair = [term[:, :128], term[:, 128:]]
    if len(refs) == 1:
        for i in range(2):
            refs[0][i] = pair[i].astype(jnp.bfloat16)
        return
    got_ref, *outs = refs
    for half, out in enumerate(outs):

        @pl.when(pl.program_id(0) == half)
        def _():
            for i in range(2):
                out[i] = (pair[i] + got_ref[i].astype(jnp.float32)).astype(jnp.bfloat16)


def input_terms(blocks, g, wq, wkv, *got):
    n_q, n_kv = wq.shape[1], wkv.shape[1]
    rows = g.shape[0]
    n = blocks.shape[0]
    one = lambda r, blocks: (blocks[2 * r], 0, 0)
    two = lambda r, blocks: (blocks[2 * r + 1], 0, 0)
    mine = lambda r, blocks: (r, 0, 0)
    fixed = lambda r, blocks: (0, 0, 0)
    block = (2, rows, 128)
    places = [fixed, fixed] if got else [mine]
    wq, wkv = wq.reshape(-1, 128, n_q), wkv.reshape(-1, 128, n_kv)
    return pl.pallas_call(
        input_body,
        grid_spec=pltpu.PrefetchScalarGridSpec(
            num_scalar_prefetch=1,
            grid=(n // 2,),
            in_specs=[
                pl.BlockSpec(g.shape, lambda r, blocks: (0, 0)),
                pl.BlockSpec((1, 128, n_q), one),
                pl.BlockSpec((1, 128, n_q), two),
                pl.BlockSpec((1, 128, n_kv), one),
                pl.BlockSpec((1, 128, n_kv), two),
            ]
            + [pl.BlockSpec(block, mine)] * len(got),
            out_specs=[pl.BlockSpec(block, place) for place in places],
        ),
        out_shape=[jax.ShapeDtypeStruct((n // len(places), rows, 128), jnp.bfloat16) for _ in places],
        compiler_params=PARAMS,
        cost_estimate=COST,
    )(blocks, g, wq, wq, wkv, wkv, *got)


def local(inputs, q_grad, key_value_share_gradient, q_weight, key_value_weight):
    q_columns = q_grad.shape[1]
    core = lax.axis_index("core")
    zhi = lax.axis_index("zhi")
    y = lax.axis_index(TOK)

    more = lax.ppermute(key_value_share_gradient, "core", SWAP)
    mine = own_rows(core.reshape(1), again(q_grad), key_value_share_gradient, more)
    far = lax.ppermute(mine, "zhi", SWAP)

    v = (y - core) % N_Y
    blocks_of = lambda at: jnp.stack(
        [second(at, jnp.where), third(second(at, jnp.where), jnp.where), at, third(at, jnp.where)]
    )
    keep_blocks = (blocks_of(v) + core) % N_Y
    give_blocks = (blocks_of(v + 1 - 2 * (v % 2)) + core) % N_Y
    zlo = lax.axis_index("zlo")
    heads = 2 * jnp.stack([zlo ^ 1, zlo ^ 3, zlo, zlo ^ 2])
    give_heads, keep_heads = heads + 1 - core, heads + core
    u = (lax.axis_index("x") - core) % 4
    place = jnp.stack([u, u ^ 1, 3 - u, (3 - u) ^ 1, zhi - core])
    place = (place + core) % 4
    orders = (place, keep_blocks, give_blocks, give_heads, keep_heads)
    near = all_along_x(again(mine))
    far, orders = lax.optimization_barrier((far, orders))
    place, keep_blocks, give_blocks, give_heads, keep_heads = orders
    combined = in_order(place, *near, *all_along_x(far))

    def along_y(terms, pairs):
        return lax.ppermute(terms, (*TOK, "core"), pairs)

    given = give_terms(give_blocks, inputs, combined)
    first, for_input = lax.optimization_barrier((given[0], combined))
    got = [along_y(part, FIRST) for part in (first, *given[1:])]
    (give,) = input_terms(give_heads, for_input, q_weight, key_value_weight)
    core_got = lax.ppermute(give, "core", SWAP)
    give, input_keep = input_terms(keep_heads, for_input, q_weight, key_value_weight, core_got)
    input_got = lax.ppermute(give, "zlo", [(i, i ^ 1) for i in range(4)])

    after = input_keep
    parts = []
    at = 0
    for part in got:
        part, _ = lax.optimization_barrier((part, after))
        give, after = keep_terms(keep_blocks, inputs, combined, part, at)
        parts += [after, along_y(give, SECOND)]
        at += part.shape[-1]
    keep, give = add_terms(*parts)
    got = along_y(give, THIRD)

    input_keep, give = add_terms(input_keep, input_got)
    input_got = lax.ppermute(give, "zlo", [(i, i ^ 2) for i in range(4)])
    return last_sums(input_keep, input_got, keep, got, q_columns)


def solution(mesh):
    fine = Mesh(
        mesh.devices.reshape(4, 2, 4, 2, 4, 2), ("th", "tl", "zlo", "core", "x", "zhi")
    )
    return jax.shard_map(
        local,
        mesh=fine,
        in_specs=(
            P(TOK, WID),
            P((*TOK, *WID), HEAD),
            P((*TOK, *WID), HEAD),
            P(WID, HEAD),
            P(WID, HEAD),
        ),
        out_specs=(P(TOK, (*WID, *HEAD)), P((*WID, *TOK), HEAD), P((*WID, *TOK), HEAD)),
        check_vma=False,
    )
```

```python
import functools

import jax
import jax.numpy as jnp
from jax import lax
from jax.experimental import pallas as pl
from jax.experimental.pallas import tpu as pltpu
from jax.sharding import Mesh
from jax.sharding import PartitionSpec as P

SWAP = [(0, 1), (1, 0)]
WID = ("x", "zhi")
TOK = ("th", "tl")
HEAD = ("zlo", "core")
N_Y = 8
N_PAIRS = 4
VMEM_LIMIT = 32 * 2**20
COST = pl.CostEstimate(flops=1, bytes_accessed=1, transcendentals=0)
LONG = pl.CostEstimate(flops=5 * 10**10, bytes_accessed=1, transcendentals=0)


def inner(v, where):
    return where((v % 4 == 1) | (v % 4 == 2), True, False)


def second(v, where):
    return where(inner(v, where), (3 - v) % N_Y, (7 - v) % N_Y)


def third(v, where):
    return where(inner(v, where), (7 - v) % N_Y, (3 - v) % N_Y)


def select(condition, one, other):
    return one if condition else other


def swapped(partner):
    return [
        ((v + core) % N_Y * 2 + core, (partner(v) + core) % N_Y * 2 + core)
        for v in range(N_Y)
        for core in range(2)
    ]


FIRST = swapped(lambda v: v ^ 1)
SECOND = swapped(lambda v: second(v, select))
THIRD = swapped(lambda v: third(v, select))
PARTS = (768, 384)


VMEM = pl.BlockSpec(memory_space=pltpu.VMEM)
SMEM = pl.BlockSpec(memory_space=pltpu.SMEM)
PARAMS = pltpu.CompilerParams(vmem_limit_bytes=VMEM_LIMIT)


def own_body(core, q_hbm, share_hbm, more_ref, out_ref, share_ref, sems):
    n_q = q_hbm.shape[1]
    q_copy = pltpu.make_async_copy(q_hbm, out_ref.at[:, pl.ds(0, n_q)], sems.at[0])
    share_copy = pltpu.make_async_copy(share_hbm, share_ref, sems.at[1])
    q_copy.start()
    share_copy.start()
    share_copy.wait()
    columns = pl.ds(pl.multiple_of(core[0] * 128, 128), 128)
    kv = share_ref[:, columns].astype(jnp.float32) + more_ref[:, columns].astype(jnp.float32)
    out_ref[:, n_q:] = kv.astype(out_ref.dtype)
    q_copy.wait()


def own_rows(core, q, share, more):
    hbm = pl.BlockSpec(memory_space=pltpu.HBM)
    return pl.pallas_call(
        own_body,
        out_shape=jax.ShapeDtypeStruct((q.shape[0], q.shape[1] + 128), q.dtype),
        in_specs=[SMEM, hbm, hbm, VMEM],
        out_specs=VMEM,
        scratch_shapes=[pltpu.VMEM(share.shape, share.dtype), pltpu.SemaphoreType.DMA((2,))],
        compiler_params=PARAMS,
        cost_estimate=COST,
    )(core, q, share, more)


def again_body(rows_ref, out_ref):
    out_ref[...] = rows_ref[...]


def again(rows):
    return pl.pallas_call(
        again_body,
        out_shape=jax.ShapeDtypeStruct(rows.shape, rows.dtype),
        in_specs=[VMEM],
        out_specs=VMEM,
        compiler_params=PARAMS,
        cost_estimate=LONG,
    )(rows)


def x_swap(rows, partner):
    pairs = [
        (core * 4 + (u + core) % 4, core * 4 + (partner(u) + core) % 4)
        for core in range(2)
        for u in range(4)
    ]
    return lax.ppermute(rows, ("core", "x"), pairs)


def all_along_x(rows):
    pair = jnp.stack([rows, x_swap(rows, lambda u: u ^ 1)])
    return pair, x_swap(pair, lambda u: 3 - u)


def order_body(place, *refs):
    *pairs, out_ref = refs
    for i, pair in enumerate(pairs):
        zhi = place[4] if i < 2 else 1 - place[4]
        for j in range(2):
            out_ref[2 * place[2 * (i % 2) + j] + zhi] = pair[j]


def in_order(place, *pairs):
    _, rows, columns = pairs[0].shape
    return pl.pallas_call(
        order_body,
        out_shape=jax.ShapeDtypeStruct((2 * len(pairs), rows, columns), pairs[0].dtype),
        in_specs=[SMEM] + [VMEM] * len(pairs),
        out_specs=VMEM,
        compiler_params=PARAMS,
        cost_estimate=COST,
    )(place, *pairs).reshape(-1, columns)


def dot(left, right, dims):
    return lax.dot_general(left, right, ((dims[:1], dims[1:]), ((), ())), preferred_element_type=jnp.float32)


def joined(blocks, x_ref):
    return jnp.concatenate(
        [x_ref[:, pl.ds(pl.multiple_of(blocks[r] * 128, 128), 128)] for r in range(N_PAIRS)], axis=1
    )


def give_body(blocks, x_ref, g_ref, *outs):
    columns = joined(blocks, x_ref)
    at = 0
    for out in outs:
        width = out.shape[-1]
        term = dot(columns, g_ref[:, at : at + width], (0, 0))
        for r in range(N_PAIRS):
            out[r] = term[r * 128 : (r + 1) * 128].astype(out.dtype)
        at += width


def give_terms(blocks, x, g):
    return pl.pallas_call(
        give_body,
        out_shape=[jax.ShapeDtypeStruct((N_PAIRS, 128, width), jnp.bfloat16) for width in PARTS],
        in_specs=[SMEM] + [VMEM] * 2,
        out_specs=[VMEM] * len(PARTS),
        compiler_params=PARAMS,
        cost_estimate=COST,
    )(blocks, x, g)


def keep_body(at, blocks, x_ref, g_ref, got_ref, give_ref, keep_ref):
    width = got_ref.shape[-1]
    term = dot(joined(blocks, x_ref), g_ref[:, at : at + width], (0, 0))
    for r in range(N_PAIRS):
        total = term[r * 128 : (r + 1) * 128] + got_ref[r].astype(jnp.float32)
        out = give_ref if r < 2 else keep_ref
        out[r % 2] = total.astype(out.dtype)


def keep_terms(blocks, x, g, got, at):
    return pl.pallas_call(
        functools.partial(keep_body, at),
        out_shape=[jax.ShapeDtypeStruct((2, *got.shape[1:]), jnp.bfloat16)] * 2,
        in_specs=[SMEM] + [VMEM] * 3,
        out_specs=[VMEM] * 2,
        compiler_params=PARAMS,
        cost_estimate=COST,
    )(blocks, x, g, got)


def add_body(*refs):
    *parts, keep_ref, give_ref = refs
    at = 0
    for kept, got in zip(parts[::2], parts[1::2]):
        width = kept.shape[-1]
        for r, out in enumerate((keep_ref, give_ref)):
            total = kept[r].astype(jnp.float32) + got[r].astype(jnp.float32)
            out[:, at : at + width] = total.astype(out.dtype)
        at += width


def add_terms(*parts):
    columns = sum(part.shape[-1] for part in parts[::2])
    return pl.pallas_call(
        add_body,
        out_shape=[jax.ShapeDtypeStruct((parts[0].shape[1], columns), jnp.bfloat16)] * 2,
        in_specs=[VMEM] * len(parts),
        out_specs=[VMEM] * 2,
        compiler_params=PARAMS,
        cost_estimate=COST,
    )(*parts)


def sum_body(input_kept, input_got, kept, got, input_out, q_ref, kv_ref):
    n_q = q_ref.shape[1]
    total = input_kept[...].astype(jnp.float32) + input_got[...].astype(jnp.float32)
    input_out[...] = total.astype(input_out.dtype)
    q_ref[...] = kept[:, :n_q].astype(jnp.float32) + got[:, :n_q].astype(jnp.float32)
    kv_ref[...] = kept[:, n_q:].astype(jnp.float32) + got[:, n_q:].astype(jnp.float32)


def last_sums(input_kept, input_got, kept, got, n_q):
    rows, columns = kept.shape
    outs = [
        jax.ShapeDtypeStruct(input_kept.shape, jnp.bfloat16),
        jax.ShapeDtypeStruct((rows, n_q), jnp.float32),
        jax.ShapeDtypeStruct((rows, columns - n_q), jnp.float32),
    ]
    block = lambda array: pl.BlockSpec(array.shape, lambda i: (0, 0))
    arrays = [input_kept, input_got, kept, got]
    return pl.pallas_call(
        sum_body,
        grid=(1,),
        out_shape=outs,
        in_specs=[block(array) for array in arrays],
        out_specs=[block(out) for out in outs],
        compiler_params=PARAMS,
        cost_estimate=COST,
    )(*arrays)


def input_body(blocks, g_ref, wq_one, wq_two, wkv_one, wkv_two, *refs):
    n_q = wq_one.shape[-1]
    wq = jnp.concatenate([wq_one[0], wq_two[0]])
    wkv = jnp.concatenate([wkv_one[0], wkv_two[0]])
    term = dot(g_ref[:, :n_q], wq, (1, 1)) + dot(g_ref[:, n_q:], wkv, (1, 1))
    pair = [term[:, :128], term[:, 128:]]
    if len(refs) == 1:
        for i in range(2):
            refs[0][i] = pair[i].astype(jnp.bfloat16)
        return
    got_ref, *outs = refs
    for half, out in enumerate(outs):

        @pl.when(pl.program_id(0) == half)
        def _():
            for i in range(2):
                out[i] = (pair[i] + got_ref[i].astype(jnp.float32)).astype(jnp.bfloat16)


def input_terms(blocks, g, wq, wkv, *got):
    n_q, n_kv = wq.shape[1], wkv.shape[1]
    rows = g.shape[0]
    n = blocks.shape[0]
    one = lambda r, blocks: (blocks[2 * r], 0, 0)
    two = lambda r, blocks: (blocks[2 * r + 1], 0, 0)
    mine = lambda r, blocks: (r, 0, 0)
    fixed = lambda r, blocks: (0, 0, 0)
    block = (2, rows, 128)
    places = [fixed, fixed] if got else [mine]
    wq, wkv = wq.reshape(-1, 128, n_q), wkv.reshape(-1, 128, n_kv)
    return pl.pallas_call(
        input_body,
        grid_spec=pltpu.PrefetchScalarGridSpec(
            num_scalar_prefetch=1,
            grid=(n // 2,),
            in_specs=[
                pl.BlockSpec(g.shape, lambda r, blocks: (0, 0)),
                pl.BlockSpec((1, 128, n_q), one),
                pl.BlockSpec((1, 128, n_q), two),
                pl.BlockSpec((1, 128, n_kv), one),
                pl.BlockSpec((1, 128, n_kv), two),
            ]
            + [pl.BlockSpec(block, mine)] * len(got),
            out_specs=[pl.BlockSpec(block, place) for place in places],
        ),
        out_shape=[jax.ShapeDtypeStruct((n // len(places), rows, 128), jnp.bfloat16) for _ in places],
        compiler_params=PARAMS,
        cost_estimate=COST,
    )(blocks, g, wq, wq, wkv, wkv, *got)


def local(inputs, q_grad, key_value_share_gradient, q_weight, key_value_weight):
    q_columns = q_grad.shape[1]
    core = lax.axis_index("core")
    zhi = lax.axis_index("zhi")
    y = lax.axis_index(TOK)

    more = lax.ppermute(key_value_share_gradient, "core", SWAP)
    mine = own_rows(core.reshape(1), again(q_grad), again(key_value_share_gradient), more)
    far = lax.ppermute(mine, "zhi", SWAP)

    v = (y - core) % N_Y
    blocks_of = lambda at: jnp.stack(
        [second(at, jnp.where), third(second(at, jnp.where), jnp.where), at, third(at, jnp.where)]
    )
    keep_blocks = (blocks_of(v) + core) % N_Y
    give_blocks = (blocks_of(v + 1 - 2 * (v % 2)) + core) % N_Y
    zlo = lax.axis_index("zlo")
    heads = 2 * jnp.stack([zlo ^ 1, zlo ^ 3, zlo, zlo ^ 2])
    give_heads, keep_heads = heads + 1 - core, heads + core
    u = (lax.axis_index("x") - core) % 4
    place = jnp.stack([u, u ^ 1, 3 - u, (3 - u) ^ 1, zhi - core])
    place = (place + core) % 4
    orders = (place, keep_blocks, give_blocks, give_heads, keep_heads)
    near = all_along_x(again(mine))
    far, orders = lax.optimization_barrier((far, orders))
    place, keep_blocks, give_blocks, give_heads, keep_heads = orders
    combined = in_order(place, *near, *all_along_x(far))

    def along_y(terms, pairs):
        return lax.ppermute(terms, (*TOK, "core"), pairs)

    given = give_terms(give_blocks, inputs, combined)
    first, for_input = lax.optimization_barrier((given[0], combined))
    got = [along_y(part, FIRST) for part in (first, *given[1:])]
    (give,) = input_terms(give_heads, for_input, q_weight, key_value_weight)
    core_got = lax.ppermute(give, "core", SWAP)
    give, input_keep = input_terms(keep_heads, for_input, q_weight, key_value_weight, core_got)
    input_got = lax.ppermute(give, "zlo", [(i, i ^ 1) for i in range(4)])

    after = input_keep
    parts = []
    at = 0
    for part in got:
        part, _ = lax.optimization_barrier((part, after))
        give, after = keep_terms(keep_blocks, inputs, combined, part, at)
        parts += [after, along_y(give, SECOND)]
        at += part.shape[-1]
    keep, give = add_terms(*parts)
    got = along_y(give, THIRD)

    input_keep, give = add_terms(input_keep, input_got)
    input_got = lax.ppermute(give, "zlo", [(i, i ^ 2) for i in range(4)])
    return last_sums(input_keep, input_got, keep, got, q_columns)


def solution(mesh):
    fine = Mesh(
        mesh.devices.reshape(4, 2, 4, 2, 4, 2), ("th", "tl", "zlo", "core", "x", "zhi")
    )
    return jax.shard_map(
        local,
        mesh=fine,
        in_specs=(
            P(TOK, WID),
            P((*TOK, *WID), HEAD),
            P((*TOK, *WID), HEAD),
            P(WID, HEAD),
            P(WID, HEAD),
        ),
        out_specs=(P(TOK, (*WID, *HEAD)), P((*WID, *TOK), HEAD), P((*WID, *TOK), HEAD)),
        check_vma=False,
    )
```

```python
import functools

import jax
import jax.numpy as jnp
from jax import lax
from jax.experimental import pallas as pl
from jax.experimental.pallas import tpu as pltpu
from jax.sharding import Mesh
from jax.sharding import PartitionSpec as P

SWAP = [(0, 1), (1, 0)]
WID = ("x", "zhi")
TOK = ("th", "tl")
HEAD = ("zlo", "core")
N_Y = 8
N_PAIRS = 4
VMEM_LIMIT = 32 * 2**20
COST = pl.CostEstimate(flops=1, bytes_accessed=1, transcendentals=0)
LONG = pl.CostEstimate(flops=5 * 10**10, bytes_accessed=1, transcendentals=0)


def inner(v, where):
    return where((v % 4 == 1) | (v % 4 == 2), True, False)


def second(v, where):
    return where(inner(v, where), (3 - v) % N_Y, (7 - v) % N_Y)


def third(v, where):
    return where(inner(v, where), (7 - v) % N_Y, (3 - v) % N_Y)


def select(condition, one, other):
    return one if condition else other


def swapped(partner):
    return [
        ((v + core) % N_Y * 2 + core, (partner(v) + core) % N_Y * 2 + core)
        for v in range(N_Y)
        for core in range(2)
    ]


FIRST = swapped(lambda v: v ^ 1)
SECOND = swapped(lambda v: second(v, select))
THIRD = swapped(lambda v: third(v, select))
PARTS = (768, 384)


VMEM = pl.BlockSpec(memory_space=pltpu.VMEM)
SMEM = pl.BlockSpec(memory_space=pltpu.SMEM)
PARAMS = pltpu.CompilerParams(vmem_limit_bytes=VMEM_LIMIT)


def own_body(core, q_hbm, share_hbm, more_ref, out_ref, share_ref, sems):
    n_q = q_hbm.shape[1]
    q_copy = pltpu.make_async_copy(q_hbm, out_ref.at[:, pl.ds(0, n_q)], sems.at[0])
    share_copy = pltpu.make_async_copy(share_hbm, share_ref, sems.at[1])
    q_copy.start()
    share_copy.start()
    share_copy.wait()
    columns = pl.ds(pl.multiple_of(core[0] * 128, 128), 128)
    kv = share_ref[:, columns].astype(jnp.float32) + more_ref[:, columns].astype(jnp.float32)
    out_ref[:, n_q:] = kv.astype(out_ref.dtype)
    q_copy.wait()


def own_rows(core, q, share, more):
    hbm = pl.BlockSpec(memory_space=pltpu.HBM)
    return pl.pallas_call(
        own_body,
        out_shape=jax.ShapeDtypeStruct((q.shape[0], q.shape[1] + 128), q.dtype),
        in_specs=[SMEM, hbm, hbm, VMEM],
        out_specs=VMEM,
        scratch_shapes=[pltpu.VMEM(share.shape, share.dtype), pltpu.SemaphoreType.DMA((2,))],
        compiler_params=PARAMS,
        cost_estimate=COST,
    )(core, q, share, more)


def again_body(rows_ref, out_ref):
    out_ref[...] = rows_ref[...]


def again(rows):
    return pl.pallas_call(
        again_body,
        out_shape=jax.ShapeDtypeStruct(rows.shape, rows.dtype),
        in_specs=[VMEM],
        out_specs=VMEM,
        compiler_params=PARAMS,
        cost_estimate=LONG,
    )(rows)


def x_swap(rows, partner):
    pairs = [
        (core * 4 + (u + core) % 4, core * 4 + (partner(u) + core) % 4)
        for core in range(2)
        for u in range(4)
    ]
    return lax.ppermute(rows, ("core", "x"), pairs)


def all_along_x(rows):
    pair = jnp.stack([rows, x_swap(rows, lambda u: u ^ 1)])
    return pair, x_swap(pair, lambda u: 3 - u)


def order_body(place, *refs):
    *pairs, out_ref = refs
    for i, pair in enumerate(pairs):
        zhi = place[4] if i < 2 else 1 - place[4]
        for j in range(2):
            out_ref[2 * place[2 * (i % 2) + j] + zhi] = pair[j]


def in_order(place, *pairs):
    _, rows, columns = pairs[0].shape
    return pl.pallas_call(
        order_body,
        out_shape=jax.ShapeDtypeStruct((2 * len(pairs), rows, columns), pairs[0].dtype),
        in_specs=[SMEM] + [VMEM] * len(pairs),
        out_specs=VMEM,
        compiler_params=PARAMS,
        cost_estimate=COST,
    )(place, *pairs).reshape(-1, columns)


def dot(left, right, dims):
    return lax.dot_general(left, right, ((dims[:1], dims[1:]), ((), ())), preferred_element_type=jnp.float32)


def joined(blocks, x_ref):
    return jnp.concatenate(
        [x_ref[:, pl.ds(pl.multiple_of(blocks[r] * 128, 128), 128)] for r in range(N_PAIRS)], axis=1
    )


def give_body(blocks, x_ref, g_ref, *outs):
    columns = joined(blocks, x_ref)
    at = 0
    for out in outs:
        width = out.shape[-1]
        term = dot(columns, g_ref[:, at : at + width], (0, 0))
        for r in range(N_PAIRS):
            out[r] = term[r * 128 : (r + 1) * 128].astype(out.dtype)
        at += width


def give_terms(blocks, x, g):
    return pl.pallas_call(
        give_body,
        out_shape=[jax.ShapeDtypeStruct((N_PAIRS, 128, width), jnp.bfloat16) for width in PARTS],
        in_specs=[SMEM] + [VMEM] * 2,
        out_specs=[VMEM] * len(PARTS),
        compiler_params=PARAMS,
        cost_estimate=COST,
    )(blocks, x, g)


def keep_body(at, blocks, x_ref, g_ref, got_ref, give_ref, keep_ref):
    width = got_ref.shape[-1]
    term = dot(joined(blocks, x_ref), g_ref[:, at : at + width], (0, 0))
    for r in range(N_PAIRS):
        total = term[r * 128 : (r + 1) * 128] + got_ref[r].astype(jnp.float32)
        out = give_ref if r < 2 else keep_ref
        out[r % 2] = total.astype(out.dtype)


def keep_terms(blocks, x, g, got, at):
    return pl.pallas_call(
        functools.partial(keep_body, at),
        out_shape=[jax.ShapeDtypeStruct((2, *got.shape[1:]), jnp.bfloat16)] * 2,
        in_specs=[SMEM] + [VMEM] * 3,
        out_specs=[VMEM] * 2,
        compiler_params=PARAMS,
        cost_estimate=COST,
    )(blocks, x, g, got)


def add_body(*refs):
    *parts, keep_ref, give_ref = refs
    at = 0
    for kept, got in zip(parts[::2], parts[1::2]):
        width = kept.shape[-1]
        for r, out in enumerate((keep_ref, give_ref)):
            total = kept[r].astype(jnp.float32) + got[r].astype(jnp.float32)
            out[:, at : at + width] = total.astype(out.dtype)
        at += width


def add_terms(*parts):
    columns = sum(part.shape[-1] for part in parts[::2])
    return pl.pallas_call(
        add_body,
        out_shape=[jax.ShapeDtypeStruct((parts[0].shape[1], columns), jnp.bfloat16)] * 2,
        in_specs=[VMEM] * len(parts),
        out_specs=[VMEM] * 2,
        compiler_params=PARAMS,
        cost_estimate=COST,
    )(*parts)


def sum_body(input_kept, input_got, kept, got, input_out, q_ref, kv_ref):
    n_q = q_ref.shape[1]
    total = input_kept[...].astype(jnp.float32) + input_got[...].astype(jnp.float32)
    input_out[...] = total.astype(input_out.dtype)
    q_ref[...] = kept[:, :n_q].astype(jnp.float32) + got[:, :n_q].astype(jnp.float32)
    kv_ref[...] = kept[:, n_q:].astype(jnp.float32) + got[:, n_q:].astype(jnp.float32)


def last_sums(input_kept, input_got, kept, got, n_q):
    rows, columns = kept.shape
    outs = [
        jax.ShapeDtypeStruct(input_kept.shape, jnp.bfloat16),
        jax.ShapeDtypeStruct((rows, n_q), jnp.float32),
        jax.ShapeDtypeStruct((rows, columns - n_q), jnp.float32),
    ]
    block = lambda array: pl.BlockSpec(array.shape, lambda i: (0, 0))
    arrays = [input_kept, input_got, kept, got]
    return pl.pallas_call(
        sum_body,
        grid=(1,),
        out_shape=outs,
        in_specs=[block(array) for array in arrays],
        out_specs=[block(out) for out in outs],
        compiler_params=PARAMS,
        cost_estimate=COST,
    )(*arrays)


def input_body(blocks, g_ref, wq_one, wq_two, wkv_one, wkv_two, *refs):
    n_q = wq_one.shape[-1]
    wq = jnp.concatenate([wq_one[0], wq_two[0]])
    wkv = jnp.concatenate([wkv_one[0], wkv_two[0]])
    term = dot(g_ref[:, :n_q], wq, (1, 1)) + dot(g_ref[:, n_q:], wkv, (1, 1))
    pair = [term[:, :128], term[:, 128:]]
    if len(refs) == 1:
        for i in range(2):
            refs[0][i] = pair[i].astype(jnp.bfloat16)
        return
    got_ref, *outs = refs
    for half, out in enumerate(outs):

        @pl.when(pl.program_id(0) == half)
        def _():
            for i in range(2):
                out[i] = (pair[i] + got_ref[i].astype(jnp.float32)).astype(jnp.bfloat16)


def input_terms(blocks, g, wq, wkv, *got):
    n_q, n_kv = wq.shape[1], wkv.shape[1]
    rows = g.shape[0]
    n = blocks.shape[0]
    one = lambda r, blocks: (blocks[2 * r], 0, 0)
    two = lambda r, blocks: (blocks[2 * r + 1], 0, 0)
    mine = lambda r, blocks: (r, 0, 0)
    fixed = lambda r, blocks: (0, 0, 0)
    block = (2, rows, 128)
    places = [fixed, fixed] if got else [mine]
    wq, wkv = wq.reshape(-1, 128, n_q), wkv.reshape(-1, 128, n_kv)
    return pl.pallas_call(
        input_body,
        grid_spec=pltpu.PrefetchScalarGridSpec(
            num_scalar_prefetch=1,
            grid=(n // 2,),
            in_specs=[
                pl.BlockSpec(g.shape, lambda r, blocks: (0, 0)),
                pl.BlockSpec((1, 128, n_q), one),
                pl.BlockSpec((1, 128, n_q), two),
                pl.BlockSpec((1, 128, n_kv), one),
                pl.BlockSpec((1, 128, n_kv), two),
            ]
            + [pl.BlockSpec(block, mine)] * len(got),
            out_specs=[pl.BlockSpec(block, place) for place in places],
        ),
        out_shape=[jax.ShapeDtypeStruct((n // len(places), rows, 128), jnp.bfloat16) for _ in places],
        compiler_params=PARAMS,
        cost_estimate=COST,
    )(blocks, g, wq, wq, wkv, wkv, *got)


def local(inputs, q_grad, key_value_share_gradient, q_weight, key_value_weight):
    q_columns = q_grad.shape[1]
    core = lax.axis_index("core")
    zhi = lax.axis_index("zhi")
    y = lax.axis_index(TOK)

    more = lax.ppermute(key_value_share_gradient, "core", SWAP)
    mine = own_rows(core.reshape(1), again(q_grad), again(key_value_share_gradient), more)
    far = lax.ppermute(mine, "zhi", SWAP)

    v = (y - core) % N_Y
    blocks_of = lambda at: jnp.stack(
        [second(at, jnp.where), third(second(at, jnp.where), jnp.where), at, third(at, jnp.where)]
    )
    keep_blocks = (blocks_of(v) + core) % N_Y
    give_blocks = (blocks_of(v + 1 - 2 * (v % 2)) + core) % N_Y
    zlo = lax.axis_index("zlo")
    heads = 2 * jnp.stack([zlo ^ 1, zlo ^ 3, zlo, zlo ^ 2])
    give_heads, keep_heads = heads + 1 - core, heads + core
    u = (lax.axis_index("x") - core) % 4
    place = jnp.stack([u, u ^ 1, 3 - u, (3 - u) ^ 1, zhi - core])
    place = (place + core) % 4
    orders = (place, keep_blocks, give_blocks, give_heads, keep_heads)
    near = all_along_x(again(mine))
    far, orders = lax.optimization_barrier((far, orders))
    place, keep_blocks, give_blocks, give_heads, keep_heads = orders
    combined = in_order(place, *near, *all_along_x(far))

    def along_y(terms, pairs):
        return lax.ppermute(terms, (*TOK, "core"), pairs)

    given = give_terms(give_blocks, inputs, combined)
    first, for_input = lax.optimization_barrier((given[0], combined))
    got = [along_y(part, FIRST) for part in (first, *given[1:])]
    (give,) = input_terms(give_heads, for_input, q_weight, key_value_weight)
    core_got = lax.ppermute(give, "core", SWAP)
    give, input_keep = input_terms(keep_heads, for_input, q_weight, key_value_weight, core_got)
    input_got = lax.ppermute(give, "zlo", [(i, i ^ 1) for i in range(4)])

    after = combined
    parts = []
    at = 0
    for part in got:
        part, _ = lax.optimization_barrier((part, after))
        give, after = keep_terms(keep_blocks, inputs, combined, part, at)
        parts += [after, along_y(give, SECOND)]
        at += part.shape[-1]
    keep, give = add_terms(*parts)
    got = along_y(give, THIRD)

    input_keep, give = add_terms(input_keep, input_got)
    input_got = lax.ppermute(give, "zlo", [(i, i ^ 2) for i in range(4)])
    return last_sums(input_keep, input_got, keep, got, q_columns)


def solution(mesh):
    fine = Mesh(
        mesh.devices.reshape(4, 2, 4, 2, 4, 2), ("th", "tl", "zlo", "core", "x", "zhi")
    )
    return jax.shard_map(
        local,
        mesh=fine,
        in_specs=(
            P(TOK, WID),
            P((*TOK, *WID), HEAD),
            P((*TOK, *WID), HEAD),
            P(WID, HEAD),
            P(WID, HEAD),
        ),
        out_specs=(P(TOK, (*WID, *HEAD)), P((*WID, *TOK), HEAD), P((*WID, *TOK), HEAD)),
        check_vma=False,
    )
```
